32 devices in a mesh: seq: 8 (over z, x), head: 4 (over y, core).
Axes of the slice: x: 2, y: 2, z: 4, core: 2. Of those that a mesh axis runs over, the one named last changes fastest.
Arguments:
- queries: bfloat16 [8192, 2048], P('seq', 'head'), may hold values from -108 to 108
- pool: bfloat16 [256, 128, 896], P('seq', 'head'), may hold values from -6 to 6
- w_key: bfloat16 [896, 2048], P(None, 'head'), may hold values from -0.1875 to 0.1875
- w_value: bfloat16 [896, 2048], P(None, 'head'), may hold values from -0.1875 to 0.1875
- out_grad: bfloat16 [8192, 2048], P('seq', 'head'), may hold values from -1.5 to 1.5
- nb_source: int32 [128, 2], replicated, may hold values from 0 to 7, all different within a row; in each aligned block of 16 rows (0 to 15, 16 to 31, ...) at most 8 rows name the same one
- nb_slot: int32 [128, 2], replicated, may hold values from 0 to 31
- nb_count: int32 [128], replicated, may hold values from 1 to 2
Outputs:
- attended: bfloat16 [8192, 2048], P('seq', 'head')
- grad_queries: bfloat16 [8192, 2048], P('seq', 'head')
- grad_pool: float32 [256, 128, 896], P('seq', 'head')
- grad_w_key: float32 [896, 2048], P(None, 'head')
- grad_w_value: float32 [896, 2048], P(None, 'head')
The draws below stay inside these ranges and needn't reach their ends.
Inputs may be any that keep to these rules, and one draw needn't show every extreme that they name: `nb_source`: for the 16 stretches of one device (aligned blocks of stretches), no encoder device is named by more than 8 entries, and in some block one is named exactly 8 times; the 2 neighbours of a stretch come from different encoder devices.
All inputs are finite; a program needn't handle non-finite values.
Results may differ from the reference program's by a relative error of at most 0.018.
The reference program's roundings to bfloat16 on the way count: a program that leaves them out, or rounds other values in their place, can miss the bound.
Values may be sent and summed in bfloat16 or wider, within the bound.
A program may use at most 128 MiB of HBM per device.

```python
import math
import jax
import jax.numpy as jnp
import numpy as np
from jax import lax

HEADS = 16
DH = 128
E = 896
STRETCH = 64
R = 128
KNB = 2
CH_DEV = 16
POOL = 32
CAP = 8
D = 2048
TOKENS = 8192
STRETCHES = 128
POOL_ALL = 256
N_SEQ = 8
N_HEAD = 4


def draw_queries(key, part):
    base = jax.random.truncated_normal(key, -6.0, 6.0, (TOKENS, D), jnp.float32)
    return base.astype(jnp.bfloat16)


def with_ends(array, key, low, high):
    extent = array.shape
    index_at = [jax.random.randint(jax.random.fold_in(key, axis), (), 0, extent[axis]) for axis in range(len(extent))]
    array = array.at[tuple(index_at)].set(low)
    longest = extent.index(max(extent))
    index_at[longest] = (index_at[longest] + 1) % extent[longest]
    return array.at[tuple(index_at)].set(high)


def block_levels(key, dims, split, low, high):
    gain = 1.0
    for dim, blocks in split:
        steps = jax.random.uniform(jax.random.fold_in(jax.random.fold_in(key, 6), dim), (blocks,), jnp.float32, low / len(split), high / len(split))
        gain = gain * jnp.repeat(jnp.exp(steps), dims[dim] // blocks).reshape((-1,) + (1,) * (len(dims) - 1 - dim))
    return gain


def shared_out(key, own, number, rows, amount, top, bound, slope):
    sequence = jax.random.permutation(key, amount)
    crowded, ordinary = load_shares(amount, rows * top, bound, slope, True), load_shares(amount, rows * top, bound, slope, False)
    places = jnp.arange(amount)

    def named(sizes, turn):
        used = int((sizes > 0).sum())
        fixed = max(1, used // 4)
        passed = fixed + (places - fixed + turn * (used - fixed)) % max(1, amount - fixed)
        return jnp.zeros((amount,), jnp.int32).at[sequence[jnp.where(places < fixed, places, passed)]].set(jnp.asarray(sizes, jnp.int32))

    sizes = jnp.where(number % 4 == 0, named(crowded, number // 4), named(ordinary, number - number // 4 - 1))
    mixed = jax.random.permutation(jax.random.fold_in(own, 3), amount)
    donor, taker = mixed[0:amount // 2 * 2:2], mixed[1:amount // 2 * 2:2]
    margin = jnp.minimum(sizes[donor] - 1, bound - sizes[taker]) // 2
    margin = jnp.where((donor == sequence[0]) | (taker == sequence[0]) | (sizes[taker] == 0), 0, jnp.maximum(margin, 0))
    passed = jax.random.randint(jax.random.fold_in(own, 4), (amount // 2,), 0, 1 << 20) % (margin + 1)
    sizes = sizes.at[donor].add(-passed).at[taker].add(passed)
    labels = jnp.searchsorted(jnp.cumsum(sizes), jnp.arange(rows * top), side="right").astype(jnp.int32)
    table = labels.reshape(top, rows).T
    table = table[jax.random.permutation(jax.random.fold_in(own, 1), rows)]
    turn = jax.random.randint(jax.random.fold_in(own, 2), (rows, 1), 0, top)
    return jnp.take_along_axis(table, (jnp.arange(top)[None, :] + turn) % top, axis=1)


def load_shares(count, total, bound, skew, full):
    weights = [(1 << 20) // math.isqrt(standing ** skew) + 1 for standing in range(1, count + 1)]
    largest = bound if full else min(bound, max(-(-total // count), total * weights[0] // sum(weights)))
    least = 1 if total - largest >= count - 1 else 0
    holding, rest = [largest] + [least] * (count - 1), total - largest - least * (count - 1)
    while rest > 0:
        movable = [i for i in range(1, count) if holding[i] < largest] or [i for i in range(1, count) if holding[i] < bound]
        whole, left = sum([weights[i] for i in movable]), rest
        for i in movable:
            more = min(bound - holding[i], max(1, left * weights[i] // whole), rest)
            holding[i] = holding[i] + more
            rest = rest - more
    return np.array(holding)


def normal_values(key, extent, spread, most, shards=(), kind=jnp.bfloat16):
    factor_of = block_levels(key, extent, shards, -0.22, 0.18) if shards else 1.0
    drawn = jax.random.normal(key, extent, jnp.float32) * spread * factor_of
    return jnp.minimum(jnp.maximum(drawn, -most), most).astype(kind)


def setup_inputs(seed: int = 0) -> dict:
    key_of = jax.random.split(jax.random.key(seed), 9)
    queries = draw_queries(jax.random.fold_in(key_of[8], 71), 0)
    pool = normal_values(key_of[1], (POOL_ALL, R, E), 1.0, 6.0, ((0, 8), (1, 4)))
    w_key = normal_values(key_of[2], (E, D), E ** -0.5, 0.1875, ((1, 4),))
    w_value = normal_values(key_of[3], (E, D), E ** -0.5, 0.1875, ((1, 4),))
    out_grad = normal_values(key_of[4], (TOKENS, D), 0.25, 1.5, ((0, 8), (1, 4)))
    nb_source_keys = jax.random.split(jax.random.fold_in(key_of[5], 1), STRETCHES // CH_DEV)
    nb_source_turns = jax.random.permutation(jax.random.fold_in(key_of[5], 3), STRETCHES // CH_DEV)
    nb_source = jax.vmap(lambda own, number: shared_out(jax.random.fold_in(key_of[5], 2), own, number, CH_DEV, N_SEQ, KNB, CAP, 2))(nb_source_keys, nb_source_turns).reshape((STRETCHES, KNB))
    nb_slot = with_ends(jax.random.randint(key_of[6], (STRETCHES, KNB), 0, POOL), jax.random.fold_in(key_of[6], 1), 0, POOL - 1).astype(jnp.int32)
    nb_count = with_ends(jax.random.randint(key_of[7], (STRETCHES,), 1, KNB + 1), jax.random.fold_in(key_of[7], 1), 1, KNB).astype(jnp.int32)
    return dict(queries=queries, pool=pool, w_key=w_key, w_value=w_value, out_grad=out_grad, nb_source=nb_source, nb_slot=nb_slot, nb_count=nb_count)


def reference(queries, pool, w_key, w_value, out_grad, nb_source, nb_slot, nb_count):
    f32 = jnp.float32
    requests = CH_DEV * KNB
    factor = 1.0 / math.sqrt(DH)
    index_table = (nb_source * POOL + nb_slot).astype(jnp.int32).reshape(N_SEQ, requests)
    query_all = queries.reshape(N_SEQ, CH_DEV, STRETCH, HEADS, DH)
    grad_all = out_grad.reshape(N_SEQ, CH_DEV, STRETCH, HEADS, DH)
    count_all = nb_count.reshape(N_SEQ, CH_DEV)
    both_weights = jnp.concatenate([w_key, w_value], axis=1).astype(f32)
    group_width = D // N_HEAD
    key_groups = w_key.astype(f32).reshape(E, N_HEAD, group_width)
    value_groups = w_value.astype(f32).reshape(E, N_HEAD, group_width)

    def per_owner(carry, inputs):
        grad_wk, grad_wv = carry
        index_row, query_blocks, grad_blocks, used_counts = inputs
        panels = pool[index_row]
        joined = jnp.einsum('jre,ec->jrc', panels.astype(f32), both_weights).astype(jnp.bfloat16)
        keys = joined[:, :, :D].reshape(CH_DEV, KNB, R, HEADS, DH)
        values = joined[:, :, D:].reshape(CH_DEV, KNB, R, HEADS, DH)
        query_f = query_blocks.astype(f32)
        grad_f = grad_blocks.astype(f32)
        keys_f = keys.astype(f32)
        values_f = values.astype(f32)
        scores = jnp.einsum('cqhd,ckrhd->chqkr', query_f, keys_f) * factor
        used_mask = (jnp.arange(KNB)[None, :] < used_counts[:, None])[:, None, None, :, None]
        masked_scores = jnp.where(used_mask, scores, -jnp.inf)
        row_max = lax.optimization_barrier(jnp.max(masked_scores, axis=(3, 4), keepdims=True))
        exp_scores = jnp.where(used_mask, jnp.exp(masked_scores - row_max), 0.0)
        soft_probs = exp_scores / lax.optimization_barrier(jnp.sum(exp_scores, axis=(3, 4), keepdims=True))
        soft_weights = soft_probs.astype(jnp.bfloat16)
        weights_f = soft_weights.astype(f32)
        attended = jnp.einsum('chqkr,ckrhd->cqhd', weights_f, values_f).astype(jnp.bfloat16)
        grad_probs = jnp.einsum('cqhd,ckrhd->chqkr', grad_f, values_f)
        row_dot = lax.optimization_barrier(jnp.sum(soft_probs * grad_probs, axis=(3, 4), keepdims=True))
        grad_scores = (soft_probs * (grad_probs - row_dot)).astype(jnp.bfloat16).astype(f32)
        grad_queries = (jnp.einsum('chqkr,ckrhd->cqhd', grad_scores, keys_f) * factor).astype(jnp.bfloat16)
        grad_keys = (jnp.einsum('chqkr,cqhd->ckrhd', grad_scores, query_f) * factor).astype(jnp.bfloat16)
        grad_values = jnp.einsum('chqkr,cqhd->ckrhd', weights_f, grad_f).astype(jnp.bfloat16)
        grad_keys = grad_keys.reshape(requests, R, N_HEAD, group_width).astype(f32)
        grad_values = grad_values.reshape(requests, R, N_HEAD, group_width).astype(f32)
        partial_sum = jnp.einsum('jrgc,egc->gjre', grad_keys, key_groups) + jnp.einsum('jrgc,egc->gjre', grad_values, value_groups)
        shares = lax.optimization_barrier(partial_sum.astype(jnp.bfloat16))
        contribution = lax.optimization_barrier(jnp.sum(shares.astype(f32), axis=0)).astype(jnp.bfloat16)
        panels_f = panels.astype(f32)
        grad_wk = grad_wk + jnp.einsum('jre,jrc->ec', panels_f, grad_keys.reshape(requests, R, D))
        grad_wv = grad_wv + jnp.einsum('jre,jrc->ec', panels_f, grad_values.reshape(requests, R, D))
        return ((grad_wk, grad_wv), (attended, grad_queries, contribution))
    start_carry = (jnp.zeros((E, D), f32), jnp.zeros((E, D), f32))
    (grad_w_key, grad_w_value), (attended, grad_queries, contributions) = lax.scan(per_owner, start_carry, (index_table, query_all, grad_all, count_all))
    flat_index = index_table.reshape(N_SEQ * requests)
    grad_pool = jnp.zeros((N_SEQ * POOL, R, E), f32).at[flat_index].add(contributions.reshape(N_SEQ * requests, R, E).astype(f32))
    return (attended.reshape(TOKENS, D), grad_queries.reshape(TOKENS, D), grad_pool, grad_w_key, grad_w_value)
```

```python
import functools
import math

import jax
import jax.numpy as jnp
from jax import lax
from jax.experimental import pallas as pl
from jax.experimental.pallas import tpu as pltpu
from jax.sharding import PartitionSpec as P

DH = 128
STRETCH = 64
KNB = 2
CH_DEV = 16
ROW_CUTS = 2
COL_CUTS = (512, 384)


def chunk_list(rows, width):
    step = rows // ROW_CUTS
    pieces = []
    for cut in range(ROW_CUTS):
        start = 0
        for cols in COL_CUTS:
            pieces.append((cut * step, step, start, cols))
            start += cols
    assert start == width
    return pieces


def attention_kernel(pieces, shards, counts, *refs):
    n = len(pieces)
    q_ref, g_ref, wk_ref, wv_ref = refs[:4]
    panels = refs[4 : 4 + n]
    att_ref, gq_ref = refs[4 + n : 6 + n]
    shares = refs[6 + n : 6 + 2 * n]
    gk_ref, gv_ref, x_ref, dk_ref, dv_ref = refs[6 + 2 * n :]
    step = pl.program_id(0)
    f32, bf16 = jnp.float32, jnp.bfloat16
    rows_full = x_ref.shape[0] // KNB

    def places(k, first, count):
        begin = k * rows_full + first * shards
        return slice(begin, begin + count * shards)

    for (first, count, start, cols), ref in zip(pieces, panels):
        block = ref[...]
        for k in range(KNB):
            x_ref[places(k, first, count), start : start + cols] = block[:, k].reshape(
                shards * count, cols
            )
    x = x_ref[...]
    keys = jnp.dot(x, wk_ref[...], preferred_element_type=f32).astype(bf16)
    values = jnp.dot(x, wv_ref[...], preferred_element_type=f32).astype(bf16)
    factor = 1.0 / math.sqrt(DH)
    used = lax.broadcasted_iota(jnp.int32, (STRETCH, KNB * rows_full), 1) < (
        counts[step] * rows_full
    )
    across = (((1,), (1,)), ((), ()))
    down = (((0,), (0,)), ((), ()))
    for h in range(q_ref.shape[1] // DH):
        cols = slice(h * DH, (h + 1) * DH)
        q, g, key, value = q_ref[:, cols], g_ref[:, cols], keys[:, cols], values[:, cols]
        scores = lax.dot_general(q, key, across, preferred_element_type=f32) * factor
        scores = jnp.where(used, scores, -jnp.inf)
        exps = jnp.exp(scores - jnp.max(scores, axis=1, keepdims=True))
        probs = exps / jnp.sum(exps, axis=1, keepdims=True)
        weights = probs.astype(bf16)
        att_ref[:, cols] = jnp.dot(weights, value, preferred_element_type=f32).astype(bf16)
        dprobs = lax.dot_general(g, value, across, preferred_element_type=f32)
        row_dot = jnp.sum(probs * dprobs, axis=1, keepdims=True)
        dscores = (probs * (dprobs - row_dot)).astype(bf16)
        gq_ref[:, cols] = (jnp.dot(dscores, key, preferred_element_type=f32) * factor).astype(bf16)
        dk_ref[:, cols] = (
            lax.dot_general(dscores, q, down, preferred_element_type=f32) * factor
        ).astype(bf16)
        dv_ref[:, cols] = lax.dot_general(weights, g, down, preferred_element_type=f32).astype(bf16)
    dk, dv = dk_ref[...], dv_ref[...]
    share = (
        lax.dot_general(dk, wk_ref[...], across, preferred_element_type=f32)
        + lax.dot_general(dv, wv_ref[...], across, preferred_element_type=f32)
    ).astype(bf16)
    for (first, count, start, cols), ref in zip(pieces, shares):
        for k in range(KNB):
            ref[:, k] = share[places(k, first, count), start : start + cols].reshape(
                shards, count, cols
            )

    @pl.when(step == 0)
    def _():
        gk_ref[...] = jnp.zeros_like(gk_ref)
        gv_ref[...] = jnp.zeros_like(gv_ref)

    gk_ref[...] += lax.dot_general(x, dk, down, preferred_element_type=f32)
    gv_ref[...] += lax.dot_general(x, dv, down, preferred_element_type=f32)


def attention(pieces, shards, counts, queries, out_grad, w_key, w_value, panels):
    tokens, width = queries.shape
    enc_width = w_key.shape[0]
    requests = CH_DEV * KNB
    rows_full = shards * sum(p[1] for p in pieces if p[2] == 0)
    token_spec = pl.BlockSpec((STRETCH, width), lambda i, c: (i, 0))
    weight_spec = pl.BlockSpec((enc_width, width), lambda i, c: (0, 0))
    piece_specs = [
        pl.BlockSpec((shards, KNB, p[1], p[3]), lambda i, c: (0, i, 0, 0)) for p in pieces
    ]
    bf16 = jnp.bfloat16
    outs = (
        [jax.ShapeDtypeStruct((tokens, width), bf16)] * 2
        + [jax.ShapeDtypeStruct((shards, requests, p[1], p[3]), bf16) for p in pieces]
        + [jax.ShapeDtypeStruct((enc_width, width), jnp.float32)] * 2
    )
    all_rows = KNB * rows_full
    flops = CH_DEV * 2 * all_rows * width * (6 * enc_width + 6 * STRETCH)
    return pl.pallas_call(
        functools.partial(attention_kernel, pieces, shards),
        grid_spec=pltpu.PrefetchScalarGridSpec(
            num_scalar_prefetch=1,
            grid=(CH_DEV,),
            in_specs=[token_spec] * 2 + [weight_spec] * 2 + piece_specs,
            out_specs=[token_spec] * 2 + piece_specs + [weight_spec] * 2,
            scratch_shapes=[
                pltpu.VMEM((all_rows, enc_width), bf16),
                pltpu.VMEM((all_rows, width), bf16),
                pltpu.VMEM((all_rows, width), bf16),
            ],
        ),
        out_shape=outs,
        compiler_params=pltpu.CompilerParams(
            dimension_semantics=("arbitrary",), vmem_limit_bytes=48 * 1024 * 1024
        ),
        cost_estimate=pl.CostEstimate(
            flops=flops, bytes_accessed=32 * 1024 * 1024, transcendentals=0
        ),
    )(counts, queries, out_grad, w_key, w_value, *panels)


def local(queries, pool, w_key, w_value, out_grad, nb_source, nb_slot, nb_count):
    f32 = jnp.float32
    bf16 = jnp.bfloat16
    seq_count = lax.axis_size("seq")
    seq_index = lax.axis_index("seq")
    shards = lax.axis_size("head")
    requests = CH_DEV * KNB
    capacity = max(2, 2 * requests // seq_count)
    slot_span = seq_count * capacity
    source_table = nb_source.reshape(seq_count, requests)
    slot_table = nb_slot.reshape(seq_count, requests)
    order_ids = jnp.arange(requests)
    matches = source_table[:, :, None] == source_table[:, None, :]
    before = order_ids[None, :] < order_ids[:, None]
    ranks = jnp.sum(jnp.logical_and(matches, before[None, :, :]), axis=2)
    places = jnp.arange(capacity)
    chosen = jnp.logical_and(
        (source_table == seq_index)[:, :, None], ranks[:, :, None] == places[None, None, :]
    )
    picked_slot = jnp.sum(jnp.where(chosen, slot_table[:, :, None], 0), axis=1).reshape(slot_span)
    filled = jnp.any(chosen, axis=1).reshape(slot_span)
    own_sources = lax.dynamic_index_in_dim(source_table, seq_index, 0, keepdims=False)
    own_ranks = lax.dynamic_index_in_dim(ranks, seq_index, 0, keepdims=False)
    positions = own_sources * capacity + own_ranks
    pool_count, rows, enc_width = pool.shape
    pieces = chunk_list(rows, enc_width)
    used_counts = lax.dynamic_slice_in_dim(nb_count, seq_index * CH_DEV, CH_DEV)

    panels = []
    for first, count, start, cols in pieces:
        part = pool[:, first : first + count, start : start + cols]
        outgoing = jnp.take(part, picked_slot, axis=0, mode="clip")
        incoming = lax.all_to_all(outgoing, "seq", split_axis=0, concat_axis=0, tiled=True)
        wanted = jnp.take(incoming, positions, axis=0, mode="clip")
        panels.append(lax.all_gather(wanted, "head", axis=0, tiled=False))

    results = attention(
        pieces, shards, used_counts, queries, out_grad, w_key, w_value, panels
    )
    attended, grad_queries = results[:2]
    shares = results[2 : 2 + len(pieces)]
    key_partial, value_partial = results[2 + len(pieces) :]

    back = positions[None, :] == jnp.arange(slot_span)[:, None]
    back_index = jnp.sum(jnp.where(back, order_ids[None, :], 0), axis=1)
    collect = jnp.logical_and(
        picked_slot[None, :] == jnp.arange(pool_count)[:, None], filled[None, :]
    ).astype(bf16)
    grads = []
    for share in shares:
        summed = lax.psum_scatter(share, "head", scatter_dimension=0, tiled=False)
        returning = jnp.take(summed, back_index, axis=0, mode="clip")
        arrived = lax.all_to_all(returning, "seq", split_axis=0, concat_axis=0, tiled=True)
        grads.append(jnp.einsum("pq,qre->pre", collect, arrived, preferred_element_type=f32))
    columns = len(COL_CUTS)
    grad_pool = jnp.concatenate(
        [
            jnp.concatenate(grads[cut * columns : (cut + 1) * columns], axis=2)
            for cut in range(ROW_CUTS)
        ],
        axis=1,
    )
    grad_w_key, grad_w_value = lax.psum((key_partial, value_partial), "seq")
    return attended, grad_queries, grad_pool, grad_w_key, grad_w_value


def solution(mesh):
    return jax.shard_map(
        local,
        mesh=mesh,
        in_specs=(
            P("seq", "head"),
            P("seq", "head", None),
            P(None, "head"),
            P(None, "head"),
            P("seq", "head"),
            P(),
            P(),
            P(),
        ),
        out_specs=(
            P("seq", "head"),
            P("seq", "head"),
            P("seq", "head", None),
            P(None, "head"),
            P(None, "head"),
        ),
        check_vma=False,
    )
```

```python
import functools
import math

import jax
import jax.numpy as jnp
from jax import lax
from jax.experimental import pallas as pl
from jax.experimental.pallas import tpu as pltpu
from jax.sharding import PartitionSpec as P

DH = 128
STRETCH = 64
KNB = 2
CH_DEV = 16
ROW_TILE = 16
COL_CUTS = (512, 384)


def chunk_list(rows, width):
    step = min(rows, ROW_TILE)
    pieces = []
    for cut in range(rows // step):
        start = 0
        for cols in COL_CUTS:
            pieces.append((cut * step, step, start, cols))
            start += cols
    assert start == width
    return pieces


def attention_kernel(pieces, shards, counts, *refs):
    n = len(pieces)
    q_ref, g_ref, wk_ref, wv_ref = refs[:4]
    panels = refs[4 : 4 + n]
    att_ref, gq_ref = refs[4 + n : 6 + n]
    shares = refs[6 + n : 6 + 2 * n]
    gk_ref, gv_ref, x_ref, dk_ref, dv_ref = refs[6 + 2 * n :]
    step = pl.program_id(0)
    f32, bf16 = jnp.float32, jnp.bfloat16
    rows_full = x_ref.shape[0] // KNB

    def places(k, first, count):
        begin = k * rows_full + first * shards
        return slice(begin, begin + count * shards)

    for (first, count, start, cols), ref in zip(pieces, panels):
        block = ref[...]
        for k in range(KNB):
            x_ref[places(k, first, count), start : start + cols] = block[:, k].reshape(
                shards * count, cols
            )
    x = x_ref[...]
    keys = jnp.dot(x, wk_ref[...], preferred_element_type=f32).astype(bf16)
    values = jnp.dot(x, wv_ref[...], preferred_element_type=f32).astype(bf16)
    factor = 1.0 / math.sqrt(DH)
    used = lax.broadcasted_iota(jnp.int32, (STRETCH, KNB * rows_full), 1) < (
        counts[step] * rows_full
    )
    across = (((1,), (1,)), ((), ()))
    down = (((0,), (0,)), ((), ()))
    for h in range(q_ref.shape[1] // DH):
        cols = slice(h * DH, (h + 1) * DH)
        q, g, key, value = q_ref[:, cols], g_ref[:, cols], keys[:, cols], values[:, cols]
        scores = lax.dot_general(q, key, across, preferred_element_type=f32) * factor
        scores = jnp.where(used, scores, -jnp.inf)
        exps = jnp.exp(scores - jnp.max(scores, axis=1, keepdims=True))
        probs = exps / jnp.sum(exps, axis=1, keepdims=True)
        weights = probs.astype(bf16)
        att_ref[:, cols] = jnp.dot(weights, value, preferred_element_type=f32).astype(bf16)
        dprobs = lax.dot_general(g, value, across, preferred_element_type=f32)
        row_dot = jnp.sum(probs * dprobs, axis=1, keepdims=True)
        dscores = (probs * (dprobs - row_dot)).astype(bf16)
        gq_ref[:, cols] = (jnp.dot(dscores, key, preferred_element_type=f32) * factor).astype(bf16)
        dk_ref[:, cols] = (
            lax.dot_general(dscores, q, down, preferred_element_type=f32) * factor
        ).astype(bf16)
        dv_ref[:, cols] = lax.dot_general(weights, g, down, preferred_element_type=f32).astype(bf16)
    dk, dv = dk_ref[...], dv_ref[...]
    share = (
        lax.dot_general(dk, wk_ref[...], across, preferred_element_type=f32)
        + lax.dot_general(dv, wv_ref[...], across, preferred_element_type=f32)
    ).astype(bf16)
    for (first, count, start, cols), ref in zip(pieces, shares):
        for k in range(KNB):
            ref[:, k] = share[places(k, first, count), start : start + cols].reshape(
                shards, count, cols
            )

    @pl.when(step == 0)
    def _():
        gk_ref[...] = jnp.zeros_like(gk_ref)
        gv_ref[...] = jnp.zeros_like(gv_ref)

    gk_ref[...] += lax.dot_general(x, dk, down, preferred_element_type=f32)
    gv_ref[...] += lax.dot_general(x, dv, down, preferred_element_type=f32)


def attention(pieces, shards, counts, queries, out_grad, w_key, w_value, panels):
    tokens, width = queries.shape
    enc_width = w_key.shape[0]
    requests = CH_DEV * KNB
    rows_full = shards * sum(p[1] for p in pieces if p[2] == 0)
    token_spec = pl.BlockSpec((STRETCH, width), lambda i, c: (i, 0))
    weight_spec = pl.BlockSpec((enc_width, width), lambda i, c: (0, 0))
    piece_specs = [
        pl.BlockSpec((shards, KNB, p[1], p[3]), lambda i, c: (0, i, 0, 0)) for p in pieces
    ]
    bf16 = jnp.bfloat16
    outs = (
        [jax.ShapeDtypeStruct((tokens, width), bf16)] * 2
        + [jax.ShapeDtypeStruct((shards, requests, p[1], p[3]), bf16) for p in pieces]
        + [jax.ShapeDtypeStruct((enc_width, width), jnp.float32)] * 2
    )
    all_rows = KNB * rows_full
    flops = CH_DEV * 2 * all_rows * width * (6 * enc_width + 6 * STRETCH)
    return pl.pallas_call(
        functools.partial(attention_kernel, pieces, shards),
        grid_spec=pltpu.PrefetchScalarGridSpec(
            num_scalar_prefetch=1,
            grid=(CH_DEV,),
            in_specs=[token_spec] * 2 + [weight_spec] * 2 + piece_specs,
            out_specs=[token_spec] * 2 + piece_specs + [weight_spec] * 2,
            scratch_shapes=[
                pltpu.VMEM((all_rows, enc_width), bf16),
                pltpu.VMEM((all_rows, width), bf16),
                pltpu.VMEM((all_rows, width), bf16),
            ],
        ),
        out_shape=outs,
        compiler_params=pltpu.CompilerParams(
            dimension_semantics=("arbitrary",), vmem_limit_bytes=48 * 1024 * 1024
        ),
        cost_estimate=pl.CostEstimate(
            flops=flops, bytes_accessed=32 * 1024 * 1024, transcendentals=0
        ),
    )(counts, queries, out_grad, w_key, w_value, *panels)


MESH = pl.DeviceIdType.MESH


def ring(axis):
    size, me = lax.axis_size(axis), lax.axis_index(axis)
    after = [lax.rem(me + o, size) for o in range(size)]
    before = [lax.rem(me + size - o, size) for o in range(size)]
    return size, me, after, before


def greet(axes):
    barrier = pltpu.get_barrier_semaphore()
    total = 0
    for axis in axes:
        size, _, after, _ = ring(axis)
        for o in range(1, size):
            pl.semaphore_signal(barrier, inc=1, device_id={axis: after[o]}, device_id_type=MESH)
        total += size - 1
    pl.semaphore_wait(barrier, total)


class Exchange:
    def __init__(self, axis, source, target, send, recv, own):
        self.size, me, after, before = ring(axis)
        self.own = pltpu.make_async_copy(source(me), target(me), own)
        others = range(1, self.size)

        def copy(o, place):
            return pltpu.make_async_remote_copy(
                src_ref=source(after[o]),
                dst_ref=target(place),
                send_sem=send.at[o],
                recv_sem=recv.at[o],
                device_id={axis: after[o]},
                device_id_type=MESH,
            )

        self.outward = [copy(o, me) for o in others]
        self.inward = [copy(o, before[o]) for o in others]

    def start(self):
        for copy in self.outward:
            copy.start()
        self.own.start()

    def wait_recv(self):
        for copy in self.inward:
            copy.wait_recv()
        self.own.wait()

    def wait_send(self):
        for copy in self.outward:
            copy.wait_send()


def fetch_kernel(pieces, capacity, picked, positions, pool, *refs):
    n = len(pieces)
    panels, outgoing, incoming, wanted = (refs[i * n : (i + 1) * n] for i in range(4))
    seq_send, seq_recv, seq_own, head_send, head_recv, head_own = refs[4 * n :]
    requests = wanted[0].shape[0]
    slots = outgoing[0].shape[0]

    def select(p):
        first, count, start, cols = pieces[p]

        def body(j, carry):
            outgoing[p][j] = pool[picked[j], first : first + count, start : start + cols]
            return carry

        lax.fori_loop(0, slots, body, 0)

    def crossing(p):
        return Exchange(
            "seq",
            lambda d: outgoing[p].at[pl.ds(d * capacity, capacity)],
            lambda d: incoming[p].at[pl.ds(d * capacity, capacity)],
            seq_send.at[p],
            seq_recv.at[p],
            seq_own.at[p],
        )

    def spreading(p):
        return Exchange(
            "head",
            lambda d: wanted[p],
            lambda d: panels[p].at[d],
            head_send.at[p],
            head_recv.at[p],
            head_own.at[p],
        )

    crossings = [crossing(p) for p in range(n)]
    spreadings = [spreading(p) for p in range(n)]
    select(0)
    greet(("seq", "head"))
    crossings[0].start()
    for p in range(1, n):
        select(p)
        if p == 1:
            crossings[p].start()
    for p in range(n):
        crossings[p].wait_recv()
        crossings[p].wait_send()
        if p + 2 < n:
            crossings[p + 2].start()

        def body(j, carry):
            wanted[p][j] = incoming[p][positions[j]]
            return carry

        lax.fori_loop(0, requests, body, 0)
        spreadings[p].start()
    for p in range(n):
        spreadings[p].wait_send()
        spreadings[p].wait_recv()


def return_kernel(pieces, capacity, back, *refs):
    n = len(pieces)
    shares, arrived, got, summed, returning = (refs[i * n : (i + 1) * n] for i in range(5))
    seq_send, seq_recv, seq_own, head_send, head_recv, head_own = refs[5 * n :]
    shards, requests = got[0].shape[:2]
    slots = returning[0].shape[0]

    def gathering(p):
        return Exchange(
            "head",
            lambda d: shares[p].at[d],
            lambda d: got[p].at[d],
            head_send.at[p],
            head_recv.at[p],
            head_own.at[p],
        )

    def crossing(p):
        return Exchange(
            "seq",
            lambda d: returning[p].at[pl.ds(d * capacity, capacity)],
            lambda d: arrived[p].at[pl.ds(d * capacity, capacity)],
            seq_send.at[p],
            seq_recv.at[p],
            seq_own.at[p],
        )

    gatherings = [gathering(p) for p in range(n)]
    crossings = [crossing(p) for p in range(n)]
    greet(("seq", "head"))
    for p in range(min(2, n)):
        gatherings[p].start()
    for p in range(n):
        gatherings[p].wait_recv()
        gatherings[p].wait_send()
        if p + 2 < n:
            gatherings[p + 2].start()

        def add(j, carry):
            total = got[p][0, j].astype(jnp.float32)
            for g in range(1, shards):
                total += got[p][g, j].astype(jnp.float32)
            summed[p][j] = total.astype(jnp.bfloat16)
            return carry

        def place(j, carry):
            returning[p][j] = summed[p][back[j]]
            return carry

        lax.fori_loop(0, requests, add, 0)
        lax.fori_loop(0, slots, place, 0)
        crossings[p].start()
    for p in range(n):
        crossings[p].wait_send()
        crossings[p].wait_recv()


def semaphores(n, seq_count, shards):
    dma = pltpu.SemaphoreType.DMA
    return [
        dma((n, seq_count)),
        dma((n, seq_count)),
        dma((n,)),
        dma((n, shards)),
        dma((n, shards)),
        dma((n,)),
    ]


def fetch(pieces, capacity, seq_count, shards, picked, positions, pool):
    bf16 = jnp.bfloat16
    slots, requests = picked.shape[0], positions.shape[0]
    smem = pl.BlockSpec(memory_space=pltpu.SMEM)
    return pl.pallas_call(
        functools.partial(fetch_kernel, pieces, capacity),
        out_shape=[jax.ShapeDtypeStruct((shards, requests, p[1], p[3]), bf16) for p in pieces],
        in_specs=[smem, smem, pl.BlockSpec(memory_space=pltpu.VMEM)],
        out_specs=[pl.BlockSpec(memory_space=pl.ANY)] * len(pieces),
        scratch_shapes=[pltpu.VMEM((slots, p[1], p[3]), bf16) for p in pieces]
        + [pltpu.VMEM((slots, p[1], p[3]), bf16) for p in pieces]
        + [pltpu.VMEM((requests, p[1], p[3]), bf16) for p in pieces]
        + semaphores(len(pieces), seq_count, shards),
        compiler_params=pltpu.CompilerParams(
            collective_id=0, has_side_effects=True, vmem_limit_bytes=40 * 1024 * 1024
        ),
        cost_estimate=pl.CostEstimate(
            flops=0, bytes_accessed=256 * 1024 * 1024, transcendentals=0
        ),
    )(picked, positions, pool)


def give_back(pieces, capacity, seq_count, shards, back, shares):
    bf16 = jnp.bfloat16
    slots, requests = back.shape[0], shares[0].shape[1]
    hbm = pl.BlockSpec(memory_space=pl.ANY)
    return pl.pallas_call(
        functools.partial(return_kernel, pieces, capacity),
        out_shape=[jax.ShapeDtypeStruct((slots, p[1], p[3]), bf16) for p in pieces],
        in_specs=[pl.BlockSpec(memory_space=pltpu.SMEM)] + [hbm] * len(pieces),
        out_specs=[hbm] * len(pieces),
        scratch_shapes=[pltpu.VMEM((shards, requests, p[1], p[3]), bf16) for p in pieces]
        + [pltpu.VMEM((requests, p[1], p[3]), bf16) for p in pieces]
        + [pltpu.VMEM((slots, p[1], p[3]), bf16) for p in pieces]
        + semaphores(len(pieces), seq_count, shards),
        compiler_params=pltpu.CompilerParams(
            collective_id=1, has_side_effects=True, vmem_limit_bytes=40 * 1024 * 1024
        ),
        cost_estimate=pl.CostEstimate(
            flops=0, bytes_accessed=256 * 1024 * 1024, transcendentals=0
        ),
    )(back, *shares)


def local(queries, pool, w_key, w_value, out_grad, nb_source, nb_slot, nb_count):
    f32 = jnp.float32
    bf16 = jnp.bfloat16
    seq_count = lax.axis_size("seq")
    seq_index = lax.axis_index("seq")
    shards = lax.axis_size("head")
    requests = CH_DEV * KNB
    capacity = max(2, 2 * requests // seq_count)
    slot_span = seq_count * capacity
    source_table = nb_source.reshape(seq_count, requests)
    slot_table = nb_slot.reshape(seq_count, requests)
    order_ids = jnp.arange(requests)
    matches = source_table[:, :, None] == source_table[:, None, :]
    before = order_ids[None, :] < order_ids[:, None]
    ranks = jnp.sum(jnp.logical_and(matches, before[None, :, :]), axis=2)
    places = jnp.arange(capacity)
    chosen = jnp.logical_and(
        (source_table == seq_index)[:, :, None], ranks[:, :, None] == places[None, None, :]
    )
    picked_slot = jnp.sum(jnp.where(chosen, slot_table[:, :, None], 0), axis=1).reshape(slot_span)
    filled = jnp.any(chosen, axis=1).reshape(slot_span)
    own_sources = lax.dynamic_index_in_dim(source_table, seq_index, 0, keepdims=False)
    own_ranks = lax.dynamic_index_in_dim(ranks, seq_index, 0, keepdims=False)
    positions = own_sources * capacity + own_ranks
    pool_count, rows, enc_width = pool.shape
    pieces = chunk_list(rows, enc_width)
    used_counts = lax.dynamic_slice_in_dim(nb_count, seq_index * CH_DEV, CH_DEV)

    panels = fetch(pieces, capacity, seq_count, shards, picked_slot, positions, pool)
    results = attention(
        pieces, shards, used_counts, queries, out_grad, w_key, w_value, panels
    )
    attended, grad_queries = results[:2]
    shares = results[2 : 2 + len(pieces)]
    key_partial, value_partial = results[2 + len(pieces) :]

    back = positions[None, :] == jnp.arange(slot_span)[:, None]
    back_index = jnp.sum(jnp.where(back, order_ids[None, :], 0), axis=1)
    collect = jnp.logical_and(
        picked_slot[None, :] == jnp.arange(pool_count)[:, None], filled[None, :]
    ).astype(bf16)
    arrived = give_back(pieces, capacity, seq_count, shards, back_index, shares)
    grads = [
        jnp.einsum("pq,qre->pre", collect, part, preferred_element_type=f32) for part in arrived
    ]
    columns = len(COL_CUTS)
    grad_pool = jnp.concatenate(
        [
            jnp.concatenate(grads[cut * columns : (cut + 1) * columns], axis=2)
            for cut in range(len(pieces) // columns)
        ],
        axis=1,
    )
    grad_w_key, grad_w_value = lax.psum((key_partial, value_partial), "seq")
    return attended, grad_queries, grad_pool, grad_w_key, grad_w_value


def solution(mesh):
    return jax.shard_map(
        local,
        mesh=mesh,
        in_specs=(
            P("seq", "head"),
            P("seq", "head", None),
            P(None, "head"),
            P(None, "head"),
            P("seq", "head"),
            P(),
            P(),
            P(),
        ),
        out_specs=(
            P("seq", "head"),
            P("seq", "head"),
            P("seq", "head", None),
            P(None, "head"),
            P(None, "head"),
        ),
        check_vma=False,
    )
```

```python
import functools
import math

import jax
import jax.numpy as jnp
from jax import lax
from jax.experimental import pallas as pl
from jax.experimental.pallas import tpu as pltpu
from jax.sharding import PartitionSpec as P

DH = 128
STRETCH = 64
KNB = 2
CH_DEV = 16
GROUP = 4
VMEM_LIMIT = 60 * 1024 * 1024
ROW_TILE = 16
COL_CUTS = (512, 384)


def chunk_list(rows, width):
    step = min(rows, ROW_TILE)
    pieces = []
    for cut in range(rows // step):
        start = 0
        for cols in COL_CUTS:
            pieces.append((cut * step, step, start, cols))
            start += cols
    assert start == width
    return pieces


def attention_kernel(pieces, shards, counts, *refs):
    n = len(pieces)
    q_ref, g_ref, wk_ref, wv_ref = refs[:4]
    panels = refs[4 : 4 + n]
    att_ref, gq_ref = refs[4 + n : 6 + n]
    shares = refs[6 + n : 6 + 2 * n]
    gw_ref, x_ref, d_ref = refs[6 + 2 * n :]
    step = pl.program_id(0)
    f32, bf16 = jnp.float32, jnp.bfloat16
    rows_full = x_ref.shape[0] // (GROUP * KNB)
    width = q_ref.shape[1]
    span = KNB * rows_full

    def places(k, first, count):
        begin = k * rows_full + first * shards
        return slice(begin, begin + count * shards)

    for (first, count, start, cols), ref in zip(pieces, panels):
        block = ref[...]
        for k in range(GROUP * KNB):
            x_ref[places(k, first, count), start : start + cols] = block[:, k].reshape(
                shards * count, cols
            )
    x = x_ref[...]
    keys = jnp.dot(x, wk_ref[...], preferred_element_type=f32).astype(bf16)
    values = jnp.dot(x, wv_ref[...], preferred_element_type=f32).astype(bf16)
    factor = 1.0 / math.sqrt(DH)
    column = lax.broadcasted_iota(jnp.int32, (STRETCH, span), 1)
    across = (((1,), (1,)), ((), ()))
    down = (((0,), (0,)), ((), ()))
    for c in range(GROUP):
        used = column < counts[step * GROUP + c] * rows_full
        tokens, rows = slice(c * STRETCH, (c + 1) * STRETCH), slice(c * span, (c + 1) * span)
        for h in range(width // DH):
            cols = slice(h * DH, (h + 1) * DH)
            q, g = q_ref[tokens, cols], g_ref[tokens, cols]
            key, value = keys[rows, cols], values[rows, cols]
            scores = lax.dot_general(q, key, across, preferred_element_type=f32) * factor
            scores = jnp.where(used, scores, -jnp.inf)
            exps = jnp.exp(scores - jnp.max(scores, axis=1, keepdims=True))
            probs = exps / jnp.sum(exps, axis=1, keepdims=True)
            weights = probs.astype(bf16)
            att_ref[tokens, cols] = jnp.dot(weights, value, preferred_element_type=f32).astype(bf16)
            dprobs = lax.dot_general(g, value, across, preferred_element_type=f32)
            row_dot = jnp.sum(probs * dprobs, axis=1, keepdims=True)
            dscores = (probs * (dprobs - row_dot)).astype(bf16)
            gq_ref[tokens, cols] = (
                jnp.dot(dscores, key, preferred_element_type=f32) * factor
            ).astype(bf16)
            d_ref[rows, cols] = (
                lax.dot_general(dscores, q, down, preferred_element_type=f32) * factor
            ).astype(bf16)
            d_ref[rows, width + h * DH : width + (h + 1) * DH] = lax.dot_general(
                weights, g, down, preferred_element_type=f32
            ).astype(bf16)
    both = d_ref[...]
    share = (
        lax.dot_general(both[:, :width], wk_ref[...], across, preferred_element_type=f32)
        + lax.dot_general(both[:, width:], wv_ref[...], across, preferred_element_type=f32)
    ).astype(bf16)
    for (first, count, start, cols), ref in zip(pieces, shares):
        for k in range(GROUP * KNB):
            ref[:, k] = share[places(k, first, count), start : start + cols].reshape(
                shards, count, cols
            )

    @pl.when(step == 0)
    def _():
        gw_ref[...] = jnp.zeros_like(gw_ref)

    partial = lax.dot_general(x, both, down, preferred_element_type=f32)
    gw_ref[0] += partial[:, :width]
    gw_ref[1] += partial[:, width:]


def attention(pieces, shards, counts, queries, out_grad, w_key, w_value, panels):
    tokens, width = queries.shape
    enc_width = w_key.shape[0]
    requests = CH_DEV * KNB
    rows_full = shards * sum(p[1] for p in pieces if p[2] == 0)
    token_spec = pl.BlockSpec((GROUP * STRETCH, width), lambda i, c: (i, 0))
    weight_spec = pl.BlockSpec((enc_width, width), lambda i, c: (0, 0))
    piece_specs = [
        pl.BlockSpec((shards, GROUP * KNB, p[1], p[3]), lambda i, c: (0, i, 0, 0)) for p in pieces
    ]
    bf16 = jnp.bfloat16
    outs = (
        [jax.ShapeDtypeStruct((tokens, width), bf16)] * 2
        + [jax.ShapeDtypeStruct((shards, requests, p[1], p[3]), bf16) for p in pieces]
        + [jax.ShapeDtypeStruct((2, enc_width, width), jnp.float32)]
    )
    all_rows = GROUP * KNB * rows_full
    flops = CH_DEV // GROUP * 2 * all_rows * width * (6 * enc_width + 6 * STRETCH)
    return pl.pallas_call(
        functools.partial(attention_kernel, pieces, shards),
        grid_spec=pltpu.PrefetchScalarGridSpec(
            num_scalar_prefetch=1,
            grid=(CH_DEV // GROUP,),
            in_specs=[token_spec] * 2 + [weight_spec] * 2 + piece_specs,
            out_specs=[token_spec] * 2
            + piece_specs
            + [pl.BlockSpec((2, enc_width, width), lambda i, c: (0, 0, 0))],
            scratch_shapes=[
                pltpu.VMEM((all_rows, enc_width), bf16),
                pltpu.VMEM((all_rows, 2 * width), bf16),
            ],
        ),
        out_shape=outs,
        compiler_params=pltpu.CompilerParams(
            dimension_semantics=("arbitrary",), vmem_limit_bytes=VMEM_LIMIT
        ),
        cost_estimate=pl.CostEstimate(
            flops=flops, bytes_accessed=32 * 1024 * 1024, transcendentals=0
        ),
    )(counts, queries, out_grad, w_key, w_value, *panels)


MESH = pl.DeviceIdType.MESH


def ring(axis):
    size, me = lax.axis_size(axis), lax.axis_index(axis)
    after = [lax.rem(me + o, size) for o in range(size)]
    before = [lax.rem(me + size - o, size) for o in range(size)]
    return size, me, after, before


def greet(axes):
    barrier = pltpu.get_barrier_semaphore()
    total = 0
    for axis in axes:
        size, _, after, _ = ring(axis)
        for o in range(1, size):
            pl.semaphore_signal(barrier, inc=1, device_id={axis: after[o]}, device_id_type=MESH)
        total += size - 1
    pl.semaphore_wait(barrier, total)


class Exchange:
    def __init__(self, axis, source, target, send, recv, own):
        self.size, me, after, before = ring(axis)
        self.own = pltpu.make_async_copy(source(me), target(me), own)
        others = range(1, self.size)

        def copy(o, place):
            return pltpu.make_async_remote_copy(
                src_ref=source(after[o]),
                dst_ref=target(place),
                send_sem=send.at[o],
                recv_sem=recv.at[o],
                device_id={axis: after[o]},
                device_id_type=MESH,
            )

        self.outward = [copy(o, me) for o in others]
        self.inward = [copy(o, before[o]) for o in others]

    def start(self):
        for copy in self.outward:
            copy.start()
        self.own.start()

    def wait_recv(self):
        for copy in self.inward:
            copy.wait_recv()
        self.own.wait()

    def wait_send(self):
        for copy in self.outward:
            copy.wait_send()


def fetch_kernel(pieces, capacity, picked, positions, pool, *refs):
    n = len(pieces)
    panels, outgoing, incoming, wanted = (refs[i * n : (i + 1) * n] for i in range(4))
    seq_send, seq_recv, seq_own, head_send, head_recv, head_own = refs[4 * n :]
    requests = wanted[0].shape[0]
    slots = outgoing[0].shape[0]

    def select(p):
        first, count, start, cols = pieces[p]

        def body(j, carry):
            outgoing[p][j] = pool[picked[j], first : first + count, start : start + cols]
            return carry

        lax.fori_loop(0, slots, body, 0)

    def crossing(p):
        return Exchange(
            "seq",
            lambda d: outgoing[p].at[pl.ds(d * capacity, capacity)],
            lambda d: incoming[p].at[pl.ds(d * capacity, capacity)],
            seq_send.at[p],
            seq_recv.at[p],
            seq_own.at[p],
        )

    def spreading(p):
        return Exchange(
            "head",
            lambda d: wanted[p],
            lambda d: panels[p].at[d],
            head_send.at[p],
            head_recv.at[p],
            head_own.at[p],
        )

    crossings = [crossing(p) for p in range(n)]
    spreadings = [spreading(p) for p in range(n)]
    select(0)
    greet(("seq", "head"))
    crossings[0].start()
    for p in range(1, n):
        select(p)
        if p == 1:
            crossings[p].start()
    for p in range(n):
        crossings[p].wait_recv()
        crossings[p].wait_send()
        if p + 2 < n:
            crossings[p + 2].start()

        def body(j, carry):
            wanted[p][j] = incoming[p][positions[j]]
            return carry

        lax.fori_loop(0, requests, body, 0)
        spreadings[p].start()
    for p in range(n):
        spreadings[p].wait_send()
        spreadings[p].wait_recv()


def return_kernel(pieces, capacity, back, partial, *refs):
    n = len(pieces)
    shares, arrived = refs[:n], refs[n : 2 * n]
    weights = refs[2 * n]
    got, summed, returning = (refs[2 * n + 1 + i * n : 2 * n + 1 + (i + 1) * n] for i in range(3))
    seq_send, seq_recv, seq_own, head_send, head_recv, head_own = refs[5 * n + 1 : 5 * n + 7]
    half, half_in, mine, mine_in, pair_sem, sum_send, sum_recv, all_send, all_recv = refs[
        5 * n + 7 :
    ]
    f32, bf16 = jnp.float32, jnp.bfloat16
    shards, requests = got[0].shape[:2]
    slots = returning[0].shape[0]

    def gathering(p):
        return Exchange(
            "head",
            lambda d: shares[p].at[d],
            lambda d: got[p].at[d],
            head_send.at[p],
            head_recv.at[p],
            head_own.at[p],
        )

    def crossing(p):
        return Exchange(
            "seq",
            lambda d: returning[p].at[pl.ds(d * capacity, capacity)],
            lambda d: arrived[p].at[pl.ds(d * capacity, capacity)],
            seq_send.at[p],
            seq_recv.at[p],
            seq_own.at[p],
        )

    me, size = lax.axis_index("seq"), lax.axis_size("seq")
    pairs = size // 2
    side, rank = lax.rem(me, 2), lax.div(me, 2)

    def to_seq(src, dst, send, recv, device):
        return pltpu.make_async_remote_copy(
            src_ref=src,
            dst_ref=dst,
            send_sem=send,
            recv_sem=recv,
            device_id={"seq": device},
            device_id_type=MESH,
        )

    def at(o):
        return lax.rem(rank + o, pairs)

    others = range(1, pairs)
    partner = 2 * rank + 1 - side
    halving = to_seq(half, half_in, pair_sem.at[0], pair_sem.at[1], partner)
    doubling = to_seq(weights.at[side], weights.at[side], pair_sem.at[2], pair_sem.at[3], partner)
    doubled = to_seq(
        weights.at[side], weights.at[1 - side], pair_sem.at[2], pair_sem.at[3], partner
    )
    sums = [
        to_seq(mine.at[at(o)], mine_in.at[o], sum_send.at[o], sum_recv.at[o], 2 * at(o) + side)
        for o in others
    ]

    def sharing(o, place):
        return to_seq(
            weights.at[side, rank],
            weights.at[side, place],
            all_send.at[o],
            all_recv.at[o],
            2 * at(o) + side,
        )

    shared_out = [sharing(o, rank) for o in others]
    shared_in = [sharing(o, at(pairs - o)) for o in others]

    def first_sum():
        halving.wait_recv()

        def body(j, carry):
            mine[j] = (partial[side, j] + half_in[j].astype(f32)).astype(bf16)
            return carry

        lax.fori_loop(0, pairs, body, 0)
        for copy in sums:
            copy.start()

    def second_sum():
        total = partial[side, rank] + half_in[rank].astype(f32)
        for o, copy in zip(others, sums):
            copy.wait_recv()
            total += mine_in[o].astype(f32)
        weights[side, rank] = total.astype(bf16)
        for copy in shared_out:
            copy.start()

    def spread_sum():
        for copy in shared_in:
            copy.wait_recv()
        for copy in shared_out:
            copy.wait_send()
        doubling.start()

    gatherings = [gathering(p) for p in range(n)]
    crossings = [crossing(p) for p in range(n)]

    def cast(j, carry):
        half[j] = partial[1 - side, j].astype(bf16)
        return carry

    lax.fori_loop(0, pairs, cast, 0)
    greet(("seq", "head"))
    halving.start()
    for p in range(min(2, n)):
        gatherings[p].start()
    first_sum()
    for p in range(n):
        gatherings[p].wait_recv()
        gatherings[p].wait_send()
        if p + 2 < n:
            gatherings[p + 2].start()

        def add(j, carry):
            total = got[p][0, j].astype(jnp.float32)
            for g in range(1, shards):
                total += got[p][g, j].astype(jnp.float32)
            summed[p][j] = total.astype(jnp.bfloat16)
            return carry

        def place(j, carry):
            returning[p][j] = summed[p][back[j]]
            return carry

        lax.fori_loop(0, requests, add, 0)
        lax.fori_loop(0, slots, place, 0)
        crossings[p].start()
        if p == (n - 1) // 2:
            second_sum()
    spread_sum()
    halving.wait_send()
    for copy in sums:
        copy.wait_send()
    for p in range(n):
        crossings[p].wait_send()
        crossings[p].wait_recv()
    doubling.wait_send()
    doubled.wait_recv()


def semaphores(n, seq_count, shards):
    dma = pltpu.SemaphoreType.DMA
    return [
        dma((n, seq_count)),
        dma((n, seq_count)),
        dma((n,)),
        dma((n, shards)),
        dma((n, shards)),
        dma((n,)),
    ]


def fetch(pieces, capacity, seq_count, shards, picked, positions, pool):
    bf16 = jnp.bfloat16
    slots, requests = picked.shape[0], positions.shape[0]
    smem = pl.BlockSpec(memory_space=pltpu.SMEM)
    return pl.pallas_call(
        functools.partial(fetch_kernel, pieces, capacity),
        out_shape=[jax.ShapeDtypeStruct((shards, requests, p[1], p[3]), bf16) for p in pieces],
        in_specs=[smem, smem, pl.BlockSpec(memory_space=pltpu.VMEM)],
        out_specs=[pl.BlockSpec(memory_space=pl.ANY)] * len(pieces),
        scratch_shapes=[pltpu.VMEM((slots, p[1], p[3]), bf16) for p in pieces]
        + [pltpu.VMEM((slots, p[1], p[3]), bf16) for p in pieces]
        + [pltpu.VMEM((requests, p[1], p[3]), bf16) for p in pieces]
        + semaphores(len(pieces), seq_count, shards),
        compiler_params=pltpu.CompilerParams(
            collective_id=0, has_side_effects=True, vmem_limit_bytes=VMEM_LIMIT
        ),
        cost_estimate=pl.CostEstimate(
            flops=0, bytes_accessed=256 * 1024 * 1024, transcendentals=0
        ),
    )(picked, positions, pool)


def give_back(pieces, capacity, seq_count, shards, back, partial, shares):
    bf16 = jnp.bfloat16
    slots, requests = back.shape[0], shares[0].shape[1]
    hbm = pl.BlockSpec(memory_space=pl.ANY)
    vmem = pl.BlockSpec(memory_space=pltpu.VMEM)
    pairs, block = partial.shape[1], partial.shape[2:]
    dma = pltpu.SemaphoreType.DMA
    return pl.pallas_call(
        functools.partial(return_kernel, pieces, capacity),
        out_shape=[jax.ShapeDtypeStruct((slots, p[1], p[3]), bf16) for p in pieces]
        + [jax.ShapeDtypeStruct(partial.shape, bf16)],
        in_specs=[pl.BlockSpec(memory_space=pltpu.SMEM), vmem] + [hbm] * len(pieces),
        out_specs=[hbm] * len(pieces) + [vmem],
        scratch_shapes=[pltpu.VMEM((shards, requests, p[1], p[3]), bf16) for p in pieces]
        + [pltpu.VMEM((requests, p[1], p[3]), bf16) for p in pieces]
        + [pltpu.VMEM((slots, p[1], p[3]), bf16) for p in pieces]
        + semaphores(len(pieces), seq_count, shards)
        + [pltpu.VMEM((pairs,) + block, bf16)] * 4
        + [dma((4,))]
        + [dma((pairs,))] * 4,
        compiler_params=pltpu.CompilerParams(
            collective_id=1, has_side_effects=True, vmem_limit_bytes=VMEM_LIMIT
        ),
        cost_estimate=pl.CostEstimate(
            flops=0, bytes_accessed=256 * 1024 * 1024, transcendentals=0
        ),
    )(back, partial, *shares)


def local(queries, pool, w_key, w_value, out_grad, nb_source, nb_slot, nb_count):
    f32 = jnp.float32
    bf16 = jnp.bfloat16
    seq_count = lax.axis_size("seq")
    seq_index = lax.axis_index("seq")
    shards = lax.axis_size("head")
    requests = CH_DEV * KNB
    capacity = max(2, 2 * requests // seq_count)
    slot_span = seq_count * capacity
    source_table = nb_source.reshape(seq_count, requests)
    slot_table = nb_slot.reshape(seq_count, requests)
    order_ids = jnp.arange(requests)
    matches = source_table[:, :, None] == source_table[:, None, :]
    before = order_ids[None, :] < order_ids[:, None]
    ranks = jnp.sum(jnp.logical_and(matches, before[None, :, :]), axis=2)
    places = jnp.arange(capacity)
    chosen = jnp.logical_and(
        (source_table == seq_index)[:, :, None], ranks[:, :, None] == places[None, None, :]
    )
    picked_slot = jnp.sum(jnp.where(chosen, slot_table[:, :, None], 0), axis=1).reshape(slot_span)
    filled = jnp.any(chosen, axis=1).reshape(slot_span)
    own_sources = lax.dynamic_index_in_dim(source_table, seq_index, 0, keepdims=False)
    own_ranks = lax.dynamic_index_in_dim(ranks, seq_index, 0, keepdims=False)
    positions = own_sources * capacity + own_ranks
    pool_count, rows, enc_width = pool.shape
    pieces = chunk_list(rows, enc_width)
    used_counts = lax.dynamic_slice_in_dim(nb_count, seq_index * CH_DEV, CH_DEV)

    panels = fetch(pieces, capacity, seq_count, shards, picked_slot, positions, pool)
    results = attention(
        pieces, shards, used_counts, queries, out_grad, w_key, w_value, panels
    )
    attended, grad_queries = results[:2]
    shares = results[2 : 2 + len(pieces)]
    partial = results[-1]
    blocks = partial.reshape(2, seq_count // 2, 2 * enc_width // seq_count, partial.shape[2])

    back = positions[None, :] == jnp.arange(slot_span)[:, None]
    back_index = jnp.sum(jnp.where(back, order_ids[None, :], 0), axis=1)
    collect = jnp.logical_and(
        picked_slot[None, :] == jnp.arange(pool_count)[:, None], filled[None, :]
    ).astype(bf16)
    *arrived, total = give_back(
        pieces, capacity, seq_count, shards, back_index, blocks, shares
    )
    grads = [
        jnp.einsum("pq,qre->pre", collect, part, preferred_element_type=f32) for part in arrived
    ]
    columns = len(COL_CUTS)
    grad_pool = jnp.concatenate(
        [
            jnp.concatenate(grads[cut * columns : (cut + 1) * columns], axis=2)
            for cut in range(len(pieces) // columns)
        ],
        axis=1,
    )
    grad_w_key, grad_w_value = total.reshape(partial.shape).astype(f32)
    return attended, grad_queries, grad_pool, grad_w_key, grad_w_value


def solution(mesh):
    return jax.shard_map(
        local,
        mesh=mesh,
        in_specs=(
            P("seq", "head"),
            P("seq", "head", None),
            P(None, "head"),
            P(None, "head"),
            P("seq", "head"),
            P(),
            P(),
            P(),
        ),
        out_specs=(
            P("seq", "head"),
            P("seq", "head"),
            P("seq", "head", None),
            P(None, "head"),
            P(None, "head"),
        ),
        check_vma=False,
    )
```

```python
import functools
import math

import jax
import jax.numpy as jnp
from jax import lax
from jax.experimental import pallas as pl
from jax.experimental.pallas import tpu as pltpu
from jax.sharding import PartitionSpec as P

DH = 128
STRETCH = 64
KNB = 2
CH_DEV = 16
GROUP = 4
VMEM_LIMIT = 60 * 1024 * 1024
ROW_TILE = 16
COL_CUTS = (128, 256, 256, 256)


def chunk_list(rows, width):
    step = min(rows, ROW_TILE)
    pieces = []
    for cut in range(rows // step):
        start = 0
        for cols in COL_CUTS if cut == 0 else COL_CUTS[::-1]:
            pieces.append((cut * step, step, start, cols))
            start += cols
        assert start == width
    return pieces


def attention_kernel(pieces, shards, counts, *refs):
    n = len(pieces)
    q_ref, g_ref, wk_ref, wv_ref = refs[:4]
    panels = refs[4 : 4 + n]
    att_ref, gq_ref = refs[4 + n : 6 + n]
    shares = refs[6 + n : 6 + 2 * n]
    gw_ref, x_ref, d_ref = refs[6 + 2 * n :]
    step = pl.program_id(0)
    f32, bf16 = jnp.float32, jnp.bfloat16
    rows_full = x_ref.shape[0] // (GROUP * KNB)
    width = q_ref.shape[1]
    span = KNB * rows_full

    def places(k, first, count):
        begin = k * rows_full + first * shards
        return slice(begin, begin + count * shards)

    for (first, count, start, cols), ref in zip(pieces, panels):
        block = ref[...]
        for k in range(GROUP * KNB):
            x_ref[places(k, first, count), start : start + cols] = block[:, k].reshape(
                shards * count, cols
            )
    x = x_ref[...]
    keys = jnp.dot(x, wk_ref[...], preferred_element_type=f32).astype(bf16)
    values = jnp.dot(x, wv_ref[...], preferred_element_type=f32).astype(bf16)
    factor = 1.0 / math.sqrt(DH)
    column = lax.broadcasted_iota(jnp.int32, (width // DH * STRETCH, span), 1)
    across = (((1,), (1,)), ((), ()))
    down = (((0,), (0,)), ((), ()))
    heads = [slice(h * DH, (h + 1) * DH) for h in range(width // DH)]
    for c in range(GROUP):
        used = column < counts[step * GROUP + c] * rows_full
        tokens, rows = slice(c * STRETCH, (c + 1) * STRETCH), slice(c * span, (c + 1) * span)
        q = [q_ref[tokens, cols] for cols in heads]
        g = [g_ref[tokens, cols] for cols in heads]
        key = [keys[rows, cols] for cols in heads]
        value = [values[rows, cols] for cols in heads]

        def products(left, right):
            return jnp.concatenate(
                [
                    lax.dot_general(a, b, across, preferred_element_type=f32)
                    for a, b in zip(left, right)
                ],
                axis=0,
            )

        scores = products(q, key) * factor
        dprobs = products(g, value)
        scores = jnp.where(used, scores, -jnp.inf)
        exps = jnp.exp(scores - jnp.max(scores, axis=1, keepdims=True))
        probs = exps / jnp.sum(exps, axis=1, keepdims=True)
        weights = probs.astype(bf16)
        row_dot = jnp.sum(probs * dprobs, axis=1, keepdims=True)
        dscores = (probs * (dprobs - row_dot)).astype(bf16)
        for h, cols in enumerate(heads):
            part = slice(h * STRETCH, (h + 1) * STRETCH)
            w, d = weights[part], dscores[part]
            att_ref[tokens, cols] = jnp.dot(w, value[h], preferred_element_type=f32).astype(bf16)
            gq_ref[tokens, cols] = (
                jnp.dot(d, key[h], preferred_element_type=f32) * factor
            ).astype(bf16)
            d_ref[rows, cols] = (
                lax.dot_general(d, q[h], down, preferred_element_type=f32) * factor
            ).astype(bf16)
            d_ref[rows, width + h * DH : width + (h + 1) * DH] = lax.dot_general(
                w, g[h], down, preferred_element_type=f32
            ).astype(bf16)
    both = d_ref[...]
    share = (
        lax.dot_general(both[:, :width], wk_ref[...], across, preferred_element_type=f32)
        + lax.dot_general(both[:, width:], wv_ref[...], across, preferred_element_type=f32)
    ).astype(bf16)
    for (first, count, start, cols), ref in zip(pieces, shares):
        for k in range(GROUP * KNB):
            ref[:, k] = share[places(k, first, count), start : start + cols].reshape(
                shards, count, cols
            )

    @pl.when(step == 0)
    def _():
        gw_ref[...] = jnp.zeros_like(gw_ref)

    partial = lax.dot_general(x, both, down, preferred_element_type=f32)
    gw_ref[0] += partial[:, :width]
    gw_ref[1] += partial[:, width:]


def attention(pieces, shards, counts, queries, out_grad, w_key, w_value, panels):
    tokens, width = queries.shape
    enc_width = w_key.shape[0]
    requests = CH_DEV * KNB
    rows_full = shards * sum(p[1] for p in pieces if p[2] == 0)
    token_spec = pl.BlockSpec((GROUP * STRETCH, width), lambda i, c: (i, 0))
    weight_spec = pl.BlockSpec((enc_width, width), lambda i, c: (0, 0))
    piece_specs = [
        pl.BlockSpec((shards, GROUP * KNB, p[1], p[3]), lambda i, c: (0, i, 0, 0)) for p in pieces
    ]
    bf16 = jnp.bfloat16
    outs = (
        [jax.ShapeDtypeStruct((tokens, width), bf16)] * 2
        + [jax.ShapeDtypeStruct((shards, requests, p[1], p[3]), bf16) for p in pieces]
        + [jax.ShapeDtypeStruct((2, enc_width, width), jnp.float32)]
    )
    all_rows = GROUP * KNB * rows_full
    flops = CH_DEV // GROUP * 2 * all_rows * width * (6 * enc_width + 6 * STRETCH)
    return pl.pallas_call(
        functools.partial(attention_kernel, pieces, shards),
        grid_spec=pltpu.PrefetchScalarGridSpec(
            num_scalar_prefetch=1,
            grid=(CH_DEV // GROUP,),
            in_specs=[token_spec] * 2 + [weight_spec] * 2 + piece_specs,
            out_specs=[token_spec] * 2
            + piece_specs
            + [pl.BlockSpec((2, enc_width, width), lambda i, c: (0, 0, 0))],
            scratch_shapes=[
                pltpu.VMEM((all_rows, enc_width), bf16),
                pltpu.VMEM((all_rows, 2 * width), bf16),
            ],
        ),
        out_shape=outs,
        compiler_params=pltpu.CompilerParams(
            dimension_semantics=("arbitrary",), vmem_limit_bytes=VMEM_LIMIT
        ),
        cost_estimate=pl.CostEstimate(
            flops=flops, bytes_accessed=32 * 1024 * 1024, transcendentals=0
        ),
    )(counts, queries, out_grad, w_key, w_value, *panels)


MESH = pl.DeviceIdType.MESH


def ring(axis):
    size, me = lax.axis_size(axis), lax.axis_index(axis)
    after = [lax.rem(me + o, size) for o in range(size)]
    before = [lax.rem(me + size - o, size) for o in range(size)]
    return size, me, after, before


def greet(axes):
    barrier = pltpu.get_barrier_semaphore()
    total = 0
    for axis in axes:
        size, _, after, _ = ring(axis)
        for o in range(1, size):
            pl.semaphore_signal(barrier, inc=1, device_id={axis: after[o]}, device_id_type=MESH)
        total += size - 1
    pl.semaphore_wait(barrier, total)


class Relay:
    def __init__(self, source, target, send, recv, own):
        size, me = lax.axis_size("head"), lax.axis_index("head")
        pairs, core, row = size // 2, lax.rem(me, 2), lax.div(me, 2)
        sibling = 2 * row + 1 - core

        def copy(src, place, sem, device):
            return pltpu.make_async_remote_copy(
                src_ref=src,
                dst_ref=target(place),
                send_sem=send.at[sem],
                recv_sem=recv.at[sem],
                device_id={"head": device},
                device_id_type=MESH,
            )

        def at(o, side):
            return 2 * lax.rem(row + o, pairs) + side

        far = range(1, pairs)
        self.own = pltpu.make_async_copy(source, target(me), own)
        self.first = [copy(source, me, 0, sibling)]
        self.first += [copy(source, me, o, at(o, core)) for o in far]
        self.arrived = [copy(source, at(pairs - o, core), o, at(o, core)) for o in far]
        self.second = [
            copy(target(at(pairs - o, core)), at(pairs - o, core), pairs + o, sibling) for o in far
        ]
        self.last = [copy(source, sibling, 0, sibling)]
        self.last += [copy(source, at(pairs - o, 1 - core), pairs + o, sibling) for o in far]

    def start(self):
        for copy in self.first:
            copy.start()
        self.own.start()

    def forward(self):
        for here, on in zip(self.arrived, self.second):
            here.wait_recv()
            on.start()

    def wait(self):
        for copy in self.last:
            copy.wait_recv()
        for copy in self.first + self.second:
            copy.wait_send()
        self.own.wait()


class Exchange:
    def __init__(self, axis, source, target, send, recv, own):
        self.size, me, after, before = ring(axis)
        self.own = pltpu.make_async_copy(source(me), target(me), own)
        others = range(1, self.size)

        def copy(o, place):
            return pltpu.make_async_remote_copy(
                src_ref=source(after[o]),
                dst_ref=target(place),
                send_sem=send.at[o],
                recv_sem=recv.at[o],
                device_id={axis: after[o]},
                device_id_type=MESH,
            )

        self.outward = [copy(o, me) for o in others]
        self.inward = [copy(o, before[o]) for o in others]

    def start(self):
        for copy in self.outward:
            copy.start()
        self.own.start()

    def wait_recv(self):
        for copy in self.inward:
            copy.wait_recv()
        self.own.wait()

    def wait_send(self):
        for copy in self.outward:
            copy.wait_send()


def fetch_kernel(pieces, capacity, picked, positions, pool, *refs):
    n = len(pieces)
    panels, outgoing, incoming, wanted = (refs[i * n : (i + 1) * n] for i in range(4))
    seq_send, seq_recv, seq_own, head_send, head_recv, head_own = refs[4 * n :]
    requests = wanted[0].shape[0]
    slots = outgoing[0].shape[0]

    def select(p):
        first, count, start, cols = pieces[p]

        def body(j, carry):
            outgoing[p][j] = pool[picked[j], first : first + count, start : start + cols]
            return carry

        lax.fori_loop(0, slots, body, 0)

    def crossing(p):
        return Exchange(
            "seq",
            lambda d: outgoing[p].at[pl.ds(d * capacity, capacity)],
            lambda d: incoming[p].at[pl.ds(d * capacity, capacity)],
            seq_send.at[p],
            seq_recv.at[p],
            seq_own.at[p],
        )

    def spreading(p):
        return Relay(
            wanted[p],
            lambda d: panels[p].at[d],
            head_send.at[p],
            head_recv.at[p],
            head_own.at[p],
        )

    crossings = [crossing(p) for p in range(n)]
    spreadings = [spreading(p) for p in range(n)]
    select(0)
    greet(("seq", "head"))
    crossings[0].start()
    for p in range(1, n):
        select(p)
        if p == 1:
            crossings[p].start()
    for p in range(n):
        crossings[p].wait_recv()
        crossings[p].wait_send()
        if p + 2 < n:
            crossings[p + 2].start()

        def body(j, carry):
            wanted[p][j] = incoming[p][positions[j]]
            return carry

        lax.fori_loop(0, requests, body, 0)
        spreadings[p].start()
        if p > 0:
            spreadings[p - 1].forward()
    spreadings[n - 1].forward()
    for p in range(n):
        spreadings[p].wait()


def return_kernel(pieces, capacity, back, partial, *refs):
    n = len(pieces)
    shares, arrived = refs[:n], refs[n : 2 * n]
    weights = refs[2 * n]
    got, summed, returning = (refs[2 * n + 1 + i * n : 2 * n + 1 + (i + 1) * n] for i in range(3))
    seq_send, seq_recv, seq_own, head_send, head_recv, head_own = refs[5 * n + 1 : 5 * n + 7]
    half, half_in, mine, mine_in, pair_sem, sum_send, sum_recv, all_send, all_recv = refs[
        5 * n + 7 :
    ]
    f32, bf16 = jnp.float32, jnp.bfloat16
    shards, requests = got[0].shape[:2]
    slots = returning[0].shape[0]

    def gathering(p):
        return Exchange(
            "head",
            lambda d: shares[p].at[d],
            lambda d: got[p].at[d],
            head_send.at[p],
            head_recv.at[p],
            head_own.at[p],
        )

    def crossing(p):
        return Exchange(
            "seq",
            lambda d: returning[p].at[pl.ds(d * capacity, capacity)],
            lambda d: arrived[p].at[pl.ds(d * capacity, capacity)],
            seq_send.at[p],
            seq_recv.at[p],
            seq_own.at[p],
        )

    me, size = lax.axis_index("seq"), lax.axis_size("seq")
    pairs = size // 2
    side, rank = lax.rem(me, 2), lax.div(me, 2)

    def to_seq(src, dst, send, recv, device):
        return pltpu.make_async_remote_copy(
            src_ref=src,
            dst_ref=dst,
            send_sem=send,
            recv_sem=recv,
            device_id={"seq": device},
            device_id_type=MESH,
        )

    def at(o):
        return lax.rem(rank + o, pairs)

    others = range(1, pairs)
    partner = 2 * rank + 1 - side
    halving = to_seq(half, half_in, pair_sem.at[0], pair_sem.at[1], partner)
    doubling = to_seq(weights.at[side], weights.at[side], pair_sem.at[2], pair_sem.at[3], partner)
    doubled = to_seq(
        weights.at[side], weights.at[1 - side], pair_sem.at[2], pair_sem.at[3], partner
    )
    sums = [
        to_seq(mine.at[at(o)], mine_in.at[o], sum_send.at[o], sum_recv.at[o], 2 * at(o) + side)
        for o in others
    ]

    def sharing(o, place):
        return to_seq(
            weights.at[side, rank],
            weights.at[side, place],
            all_send.at[o],
            all_recv.at[o],
            2 * at(o) + side,
        )

    shared_out = [sharing(o, rank) for o in others]
    shared_in = [sharing(o, at(pairs - o)) for o in others]

    def first_sum():
        halving.wait_recv()

        def body(j, carry):
            mine[j] = (partial[side, j] + half_in[j].astype(f32)).astype(bf16)
            return carry

        lax.fori_loop(0, pairs, body, 0)
        for copy in sums:
            copy.start()

    def second_sum():
        total = partial[side, rank] + half_in[rank].astype(f32)
        for o, copy in zip(others, sums):
            copy.wait_recv()
            total += mine_in[o].astype(f32)
        weights[side, rank] = total.astype(bf16)
        for copy in shared_out:
            copy.start()

    def spread_sum():
        for copy in shared_in:
            copy.wait_recv()
        for copy in shared_out:
            copy.wait_send()
        doubling.start()

    gatherings = [gathering(p) for p in range(n)]
    crossings = [crossing(p) for p in range(n)]

    def cast(j, carry):
        half[j] = partial[1 - side, j].astype(bf16)
        return carry

    lax.fori_loop(0, pairs, cast, 0)
    greet(("seq", "head"))
    halving.start()
    gatherings[0].start()
    for p in range(n):
        gatherings[p].wait_recv()
        gatherings[p].wait_send()
        for later in (1, 2) if p == 0 else (p + 2,):
            if later < n:
                gatherings[later].start()

        def add(j, carry):
            total = got[p][0, j].astype(jnp.float32)
            for g in range(1, shards):
                total += got[p][g, j].astype(jnp.float32)
            summed[p][j] = total.astype(jnp.bfloat16)
            return carry

        def place(j, carry):
            returning[p][j] = summed[p][back[j]]
            return carry

        lax.fori_loop(0, requests, add, 0)
        lax.fori_loop(0, slots, place, 0)
        crossings[p].start()
        if p == 0:
            first_sum()
        if p == (n - 1) // 2:
            second_sum()
    spread_sum()
    halving.wait_send()
    for copy in sums:
        copy.wait_send()
    for p in range(n):
        crossings[p].wait_send()
        crossings[p].wait_recv()
    doubling.wait_send()
    doubled.wait_recv()


def semaphores(n, seq_count, shards):
    dma = pltpu.SemaphoreType.DMA
    return [
        dma((n, seq_count)),
        dma((n, seq_count)),
        dma((n,)),
        dma((n, shards)),
        dma((n, shards)),
        dma((n,)),
    ]


def fetch(pieces, capacity, seq_count, shards, picked, positions, pool):
    bf16 = jnp.bfloat16
    slots, requests = picked.shape[0], positions.shape[0]
    smem = pl.BlockSpec(memory_space=pltpu.SMEM)
    return pl.pallas_call(
        functools.partial(fetch_kernel, pieces, capacity),
        out_shape=[jax.ShapeDtypeStruct((shards, requests, p[1], p[3]), bf16) for p in pieces],
        in_specs=[smem, smem, pl.BlockSpec(memory_space=pltpu.VMEM)],
        out_specs=[pl.BlockSpec(memory_space=pl.ANY)] * len(pieces),
        scratch_shapes=[pltpu.VMEM((slots, p[1], p[3]), bf16) for p in pieces]
        + [pltpu.VMEM((slots, p[1], p[3]), bf16) for p in pieces]
        + [pltpu.VMEM((requests, p[1], p[3]), bf16) for p in pieces]
        + semaphores(len(pieces), seq_count, shards),
        compiler_params=pltpu.CompilerParams(
            collective_id=0, has_side_effects=True, vmem_limit_bytes=VMEM_LIMIT
        ),
        cost_estimate=pl.CostEstimate(
            flops=0, bytes_accessed=256 * 1024 * 1024, transcendentals=0
        ),
    )(picked, positions, pool)


def give_back(pieces, capacity, seq_count, shards, back, partial, shares):
    bf16 = jnp.bfloat16
    slots, requests = back.shape[0], shares[0].shape[1]
    hbm = pl.BlockSpec(memory_space=pl.ANY)
    vmem = pl.BlockSpec(memory_space=pltpu.VMEM)
    pairs, block = partial.shape[1], partial.shape[2:]
    dma = pltpu.SemaphoreType.DMA
    return pl.pallas_call(
        functools.partial(return_kernel, pieces, capacity),
        out_shape=[jax.ShapeDtypeStruct((slots, p[1], p[3]), bf16) for p in pieces]
        + [jax.ShapeDtypeStruct(partial.shape, bf16)],
        in_specs=[pl.BlockSpec(memory_space=pltpu.SMEM), vmem] + [hbm] * len(pieces),
        out_specs=[hbm] * len(pieces) + [vmem],
        scratch_shapes=[pltpu.VMEM((shards, requests, p[1], p[3]), bf16) for p in pieces]
        + [pltpu.VMEM((requests, p[1], p[3]), bf16) for p in pieces]
        + [pltpu.VMEM((slots, p[1], p[3]), bf16) for p in pieces]
        + semaphores(len(pieces), seq_count, shards)
        + [pltpu.VMEM((pairs,) + block, bf16)] * 4
        + [dma((4,))]
        + [dma((pairs,))] * 4,
        compiler_params=pltpu.CompilerParams(
            collective_id=1, has_side_effects=True, vmem_limit_bytes=VMEM_LIMIT
        ),
        cost_estimate=pl.CostEstimate(
            flops=0, bytes_accessed=256 * 1024 * 1024, transcendentals=0
        ),
    )(back, partial, *shares)


def local(queries, pool, w_key, w_value, out_grad, nb_source, nb_slot, nb_count):
    f32 = jnp.float32
    bf16 = jnp.bfloat16
    seq_count = lax.axis_size("seq")
    seq_index = lax.axis_index("seq")
    shards = lax.axis_size("head")
    requests = CH_DEV * KNB
    capacity = max(2, 2 * requests // seq_count)
    slot_span = seq_count * capacity
    source_table = nb_source.reshape(seq_count, requests)
    slot_table = nb_slot.reshape(seq_count, requests)
    order_ids = jnp.arange(requests)
    matches = source_table[:, :, None] == source_table[:, None, :]
    before = order_ids[None, :] < order_ids[:, None]
    ranks = jnp.sum(jnp.logical_and(matches, before[None, :, :]), axis=2)
    places = jnp.arange(capacity)
    chosen = jnp.logical_and(
        (source_table == seq_index)[:, :, None], ranks[:, :, None] == places[None, None, :]
    )
    picked_slot = jnp.sum(jnp.where(chosen, slot_table[:, :, None], 0), axis=1).reshape(slot_span)
    filled = jnp.any(chosen, axis=1).reshape(slot_span)
    own_sources = lax.dynamic_index_in_dim(source_table, seq_index, 0, keepdims=False)
    own_ranks = lax.dynamic_index_in_dim(ranks, seq_index, 0, keepdims=False)
    positions = own_sources * capacity + own_ranks
    pool_count, rows, enc_width = pool.shape
    pieces = chunk_list(rows, enc_width)
    used_counts = lax.dynamic_slice_in_dim(nb_count, seq_index * CH_DEV, CH_DEV)

    panels = fetch(pieces, capacity, seq_count, shards, picked_slot, positions, pool)
    results = attention(
        pieces, shards, used_counts, queries, out_grad, w_key, w_value, panels
    )
    attended, grad_queries = results[:2]
    shares = results[2 : 2 + len(pieces)]
    partial = results[-1]
    blocks = partial.reshape(2, seq_count // 2, 2 * enc_width // seq_count, partial.shape[2])

    back = positions[None, :] == jnp.arange(slot_span)[:, None]
    back_index = jnp.sum(jnp.where(back, order_ids[None, :], 0), axis=1)
    collect = jnp.logical_and(
        picked_slot[None, :] == jnp.arange(pool_count)[:, None], filled[None, :]
    ).astype(bf16)
    *arrived, total = give_back(
        pieces, capacity, seq_count, shards, back_index, blocks, shares
    )
    grads = [
        jnp.einsum("pq,qre->pre", collect, part, preferred_element_type=f32) for part in arrived
    ]
    columns = len(COL_CUTS)
    grad_pool = jnp.concatenate(
        [
            jnp.concatenate(grads[cut * columns : (cut + 1) * columns], axis=2)
            for cut in range(len(pieces) // columns)
        ],
        axis=1,
    )
    grad_w_key, grad_w_value = total.reshape(partial.shape).astype(f32)
    return attended, grad_queries, grad_pool, grad_w_key, grad_w_value


def solution(mesh):
    return jax.shard_map(
        local,
        mesh=mesh,
        in_specs=(
            P("seq", "head"),
            P("seq", "head", None),
            P(None, "head"),
            P(None, "head"),
            P("seq", "head"),
            P(),
            P(),
            P(),
        ),
        out_specs=(
            P("seq", "head"),
            P("seq", "head"),
            P("seq", "head", None),
            P(None, "head"),
            P(None, "head"),
        ),
        check_vma=False,
    )
```

```python
import functools
import math

import jax
import jax.numpy as jnp
from jax import lax
from jax.experimental import pallas as pl
from jax.experimental.pallas import tpu as pltpu
from jax.sharding import PartitionSpec as P

DH = 128
STRETCH = 64
KNB = 2
CH_DEV = 16
GROUP = 4
VMEM_LIMIT = 60 * 1024 * 1024
ROW_TILE = 16
COL_CUTS = (128, 256, 256, 256)


def chunk_list(rows, width):
    step = min(rows, ROW_TILE)
    pieces = []
    for cut in range(rows // step):
        start = 0
        for cols in COL_CUTS if cut == 0 else COL_CUTS[::-1]:
            pieces.append((cut * step, step, start, cols))
            start += cols
        assert start == width
    return pieces


def attention_kernel(pieces, shards, counts, *refs):
    n = len(pieces)
    q_ref, g_ref, wk_ref, wv_ref = refs[:4]
    panels = refs[4 : 4 + n]
    att_ref, gq_ref = refs[4 + n : 6 + n]
    shares = refs[6 + n : 6 + 2 * n]
    gw_ref, x_ref, d_ref = refs[6 + 2 * n :]
    step = pl.program_id(0)
    f32, bf16 = jnp.float32, jnp.bfloat16
    rows_full = x_ref.shape[0] // (GROUP * KNB)
    width = q_ref.shape[1]
    span = KNB * rows_full

    def places(k, first, count):
        begin = k * rows_full + first * shards
        return slice(begin, begin + count * shards)

    for (first, count, start, cols), ref in zip(pieces, panels):
        block = ref[...]
        for k in range(GROUP * KNB):
            x_ref[places(k, first, count), start : start + cols] = block[:, k].reshape(
                shards * count, cols
            )
    x = x_ref[...]
    keys = jnp.dot(x, wk_ref[...], preferred_element_type=f32).astype(bf16)
    values = jnp.dot(x, wv_ref[...], preferred_element_type=f32).astype(bf16)
    factor = 1.0 / math.sqrt(DH)
    column = lax.broadcasted_iota(jnp.int32, (width // DH * STRETCH, span), 1)
    across = (((1,), (1,)), ((), ()))
    down = (((0,), (0,)), ((), ()))
    heads = [slice(h * DH, (h + 1) * DH) for h in range(width // DH)]
    for c in range(GROUP):
        used = column < counts[step * GROUP + c] * rows_full
        tokens, rows = slice(c * STRETCH, (c + 1) * STRETCH), slice(c * span, (c + 1) * span)
        q = [q_ref[tokens, cols] for cols in heads]
        g = [g_ref[tokens, cols] for cols in heads]
        key = [keys[rows, cols] for cols in heads]
        value = [values[rows, cols] for cols in heads]

        def products(left, right):
            return jnp.concatenate(
                [
                    lax.dot_general(a, b, across, preferred_element_type=f32)
                    for a, b in zip(left, right)
                ],
                axis=0,
            )

        scores = products(q, key) * factor
        dprobs = products(g, value)
        scores = jnp.where(used, scores, -jnp.inf)
        exps = jnp.exp(scores - jnp.max(scores, axis=1, keepdims=True))
        probs = exps / jnp.sum(exps, axis=1, keepdims=True)
        weights = probs.astype(bf16)
        row_dot = jnp.sum(probs * dprobs, axis=1, keepdims=True)
        dscores = (probs * (dprobs - row_dot)).astype(bf16)
        for h, cols in enumerate(heads):
            part = slice(h * STRETCH, (h + 1) * STRETCH)
            w, d = weights[part], dscores[part]
            att_ref[tokens, cols] = jnp.dot(w, value[h], preferred_element_type=f32).astype(bf16)
            gq_ref[tokens, cols] = (
                jnp.dot(d, key[h], preferred_element_type=f32) * factor
            ).astype(bf16)
            d_ref[rows, cols] = (
                lax.dot_general(d, q[h], down, preferred_element_type=f32) * factor
            ).astype(bf16)
            d_ref[rows, width + h * DH : width + (h + 1) * DH] = lax.dot_general(
                w, g[h], down, preferred_element_type=f32
            ).astype(bf16)
    both = d_ref[...]
    share = (
        lax.dot_general(both[:, :width], wk_ref[...], across, preferred_element_type=f32)
        + lax.dot_general(both[:, width:], wv_ref[...], across, preferred_element_type=f32)
    ).astype(bf16)
    for (first, count, start, cols), ref in zip(pieces, shares):
        for k in range(GROUP * KNB):
            ref[:, k] = share[places(k, first, count), start : start + cols].reshape(
                shards, count, cols
            )

    @pl.when(step == 0)
    def _():
        gw_ref[...] = jnp.zeros_like(gw_ref)

    partial = lax.dot_general(x, both, down, preferred_element_type=f32)
    gw_ref[0] += partial[:, :width]
    gw_ref[1] += partial[:, width:]


def attention(pieces, shards, counts, queries, out_grad, w_key, w_value, panels):
    tokens, width = queries.shape
    enc_width = w_key.shape[0]
    requests = CH_DEV * KNB
    rows_full = shards * sum(p[1] for p in pieces if p[2] == 0)
    token_spec = pl.BlockSpec((GROUP * STRETCH, width), lambda i, c: (i, 0))
    weight_spec = pl.BlockSpec((enc_width, width), lambda i, c: (0, 0))
    piece_specs = [
        pl.BlockSpec((shards, GROUP * KNB, p[1], p[3]), lambda i, c: (0, i, 0, 0)) for p in pieces
    ]
    bf16 = jnp.bfloat16
    outs = (
        [jax.ShapeDtypeStruct((tokens, width), bf16)] * 2
        + [jax.ShapeDtypeStruct((shards, requests, p[1], p[3]), bf16) for p in pieces]
        + [jax.ShapeDtypeStruct((2, enc_width, width), jnp.float32)]
    )
    all_rows = GROUP * KNB * rows_full
    flops = CH_DEV // GROUP * 2 * all_rows * width * (6 * enc_width + 6 * STRETCH)
    return pl.pallas_call(
        functools.partial(attention_kernel, pieces, shards),
        grid_spec=pltpu.PrefetchScalarGridSpec(
            num_scalar_prefetch=1,
            grid=(CH_DEV // GROUP,),
            in_specs=[token_spec] * 2 + [weight_spec] * 2 + piece_specs,
            out_specs=[token_spec] * 2
            + piece_specs
            + [pl.BlockSpec((2, enc_width, width), lambda i, c: (0, 0, 0))],
            scratch_shapes=[
                pltpu.VMEM((all_rows, enc_width), bf16),
                pltpu.VMEM((all_rows, 2 * width), bf16),
            ],
        ),
        out_shape=outs,
        compiler_params=pltpu.CompilerParams(
            dimension_semantics=("arbitrary",), vmem_limit_bytes=VMEM_LIMIT
        ),
        cost_estimate=pl.CostEstimate(
            flops=flops, bytes_accessed=32 * 1024 * 1024, transcendentals=0
        ),
    )(counts, queries, out_grad, w_key, w_value, *panels)


MESH = pl.DeviceIdType.MESH


def ring(axis):
    size, me = lax.axis_size(axis), lax.axis_index(axis)
    after = [lax.rem(me + o, size) for o in range(size)]
    before = [lax.rem(me + size - o, size) for o in range(size)]
    return size, me, after, before


def greet(axes):
    barrier = pltpu.get_barrier_semaphore()
    total = 0
    for axis in axes:
        size, _, after, _ = ring(axis)
        for o in range(1, size):
            pl.semaphore_signal(barrier, inc=1, device_id={axis: after[o]}, device_id_type=MESH)
        total += size - 1
    pl.semaphore_wait(barrier, total)


class Relay:
    def __init__(self, source, target, send, recv, own):
        size, me = lax.axis_size("head"), lax.axis_index("head")
        pairs, core, row = size // 2, lax.rem(me, 2), lax.div(me, 2)
        sibling = 2 * row + 1 - core

        def copy(src, place, sem, device):
            return pltpu.make_async_remote_copy(
                src_ref=src,
                dst_ref=target(place),
                send_sem=send.at[sem],
                recv_sem=recv.at[sem],
                device_id={"head": device},
                device_id_type=MESH,
            )

        def at(o, side):
            return 2 * lax.rem(row + o, pairs) + side

        far = range(1, pairs)
        self.own = pltpu.make_async_copy(source, target(me), own)
        self.first = [copy(source, me, 0, sibling)]
        self.first += [copy(source, me, o, at(o, core)) for o in far]
        self.arrived = [copy(source, at(pairs - o, core), o, at(o, core)) for o in far]
        self.second = [
            copy(target(at(pairs - o, core)), at(pairs - o, core), pairs + o, sibling) for o in far
        ]
        self.last = [copy(source, sibling, 0, sibling)]
        self.last += [copy(source, at(pairs - o, 1 - core), pairs + o, sibling) for o in far]

    def start(self):
        for copy in self.first:
            copy.start()
        self.own.start()

    def forward(self):
        for here, on in zip(self.arrived, self.second):
            here.wait_recv()
            on.start()

    def wait(self):
        for copy in self.last:
            copy.wait_recv()
        for copy in self.first + self.second:
            copy.wait_send()
        self.own.wait()


class Exchange:
    def __init__(self, axis, source, target, send, recv, own):
        self.size, me, after, before = ring(axis)
        self.own = pltpu.make_async_copy(source(me), target(me), own)
        others = range(1, self.size)

        def copy(o, place):
            return pltpu.make_async_remote_copy(
                src_ref=source(after[o]),
                dst_ref=target(place),
                send_sem=send.at[o],
                recv_sem=recv.at[o],
                device_id={axis: after[o]},
                device_id_type=MESH,
            )

        self.outward = [copy(o, me) for o in others]
        self.inward = [copy(o, before[o]) for o in others]

    def start(self):
        for copy in self.outward:
            copy.start()
        self.own.start()

    def wait_recv(self):
        for copy in self.inward:
            copy.wait_recv()
        self.own.wait()

    def wait_send(self):
        for copy in self.outward:
            copy.wait_send()


def fetch_kernel(pieces, capacity, picked, positions, pool, *refs):
    n = len(pieces)
    panels, outgoing, incoming, wanted = (refs[i * n : (i + 1) * n] for i in range(4))
    seq_send, seq_recv, seq_own, head_send, head_recv, head_own = refs[4 * n :]
    requests = wanted[0].shape[0]
    slots = outgoing[0].shape[0]

    def select(p):
        first, count, start, cols = pieces[p]

        def body(j, carry):
            outgoing[p][j] = pool[picked[j], first : first + count, start : start + cols]
            return carry

        lax.fori_loop(0, slots, body, 0)

    def crossing(p):
        return Exchange(
            "seq",
            lambda d: outgoing[p].at[pl.ds(d * capacity, capacity)],
            lambda d: incoming[p].at[pl.ds(d * capacity, capacity)],
            seq_send.at[p],
            seq_recv.at[p],
            seq_own.at[p],
        )

    def spreading(p):
        return Relay(
            wanted[p],
            lambda d: panels[p].at[d],
            head_send.at[p],
            head_recv.at[p],
            head_own.at[p],
        )

    crossings = [crossing(p) for p in range(n)]
    spreadings = [spreading(p) for p in range(n)]
    select(0)
    greet(("seq", "head"))
    crossings[0].start()
    for p in range(1, n):
        select(p)
        if p == 1:
            crossings[p].start()
    for p in range(n):
        crossings[p].wait_recv()
        crossings[p].wait_send()
        if p + 2 < n:
            crossings[p + 2].start()

        def body(j, carry):
            wanted[p][j] = incoming[p][positions[j]]
            return carry

        lax.fori_loop(0, requests, body, 0)
        spreadings[p].start()
        if p > 0:
            spreadings[p - 1].forward()
    spreadings[n - 1].forward()
    for p in range(n):
        spreadings[p].wait()


def return_kernel(pieces, capacity, back, partial, *refs):
    n = len(pieces)
    shares, arrived = refs[:n], refs[n : 2 * n]
    weights = refs[2 * n]
    got, summed, returning = (refs[2 * n + 1 + i * n : 2 * n + 1 + (i + 1) * n] for i in range(3))
    seq_send, seq_recv, seq_own, head_send, head_recv, head_own = refs[5 * n + 1 : 5 * n + 7]
    half, half_in, mine, running, mine_in, pair_sem, sum_send, sum_recv, all_send, all_recv = refs[
        5 * n + 7 :
    ]
    f32, bf16 = jnp.float32, jnp.bfloat16
    shards, requests = got[0].shape[:2]
    slots = returning[0].shape[0]

    def gathering(p):
        return Exchange(
            "head",
            lambda d: shares[p].at[d],
            lambda d: got[p].at[d],
            head_send.at[p],
            head_recv.at[p],
            head_own.at[p],
        )

    def crossing(p):
        return Exchange(
            "seq",
            lambda d: returning[p].at[pl.ds(d * capacity, capacity)],
            lambda d: arrived[p].at[pl.ds(d * capacity, capacity)],
            seq_send.at[p],
            seq_recv.at[p],
            seq_own.at[p],
        )

    me, size = lax.axis_index("seq"), lax.axis_size("seq")
    pairs = size // 2
    side, rank = lax.rem(me, 2), lax.div(me, 2)

    def to_seq(src, dst, send, recv, device):
        return pltpu.make_async_remote_copy(
            src_ref=src,
            dst_ref=dst,
            send_sem=send,
            recv_sem=recv,
            device_id={"seq": device},
            device_id_type=MESH,
        )

    partner = 2 * rank + 1 - side
    halving = to_seq(half, half_in, pair_sem.at[0], pair_sem.at[1], partner)
    doubling = to_seq(weights.at[side], weights.at[side], pair_sem.at[2], pair_sem.at[3], partner)
    doubled = to_seq(
        weights.at[side], weights.at[1 - side], pair_sem.at[2], pair_sem.at[3], partner
    )
    levels, bit, taken = [], 1, 0
    while bit < pairs:
        near, away = lax.rem(rank, 2 * bit), lax.rem(rank + bit, 2 * bit)
        device = 2 * (rank - near + away) + side
        steps = [2 * bit * m for m in range(pairs // (2 * bit))]
        kept, given = [near + m for m in steps], [away + m for m in steps]
        box = mine_in.at[len(levels)]

        def summing(places):
            return [
                to_seq(mine.at[j], box.at[j], sum_send.at[k], sum_recv.at[k], device)
                for k, j in enumerate(places, taken)
            ]

        def sharing(places):
            return [
                to_seq(
                    weights.at[side, j], weights.at[side, j], all_send.at[k], all_recv.at[k], device
                )
                for k, j in enumerate(places, taken)
            ]

        levels.append(
            (kept, box, summing(given), summing(kept), sharing(kept), sharing(given))
        )
        taken += len(steps)
        bit *= 2

    def first_sum():
        halving.wait_recv()

        def body(j, carry):
            total = partial[side, j] + half_in[j].astype(f32)
            running[j] = total
            mine[j] = total.astype(bf16)
            return carry

        lax.fori_loop(0, pairs, body, 0)
        for copy in levels[0][2]:
            copy.start()

    def level_sum(i):
        kept, box, _, inward = levels[i][:4]
        for j, copy in zip(kept, inward):
            copy.wait_recv()
            total = running[j] + box[j].astype(f32)
            running[j] = total
            mine[j] = total.astype(bf16)
        if i + 1 < len(levels):
            for copy in levels[i + 1][2]:
                copy.start()
        else:
            weights[side, rank] = mine[rank]
            for copy in levels[i][4]:
                copy.start()

    def level_share(i):
        for copy in levels[i][5]:
            copy.wait_recv()
        if i > 0:
            for copy in levels[i - 1][4]:
                copy.start()
        else:
            doubling.start()

    actions = [first_sum]
    actions += [functools.partial(level_sum, i) for i in range(len(levels))]
    actions += [functools.partial(level_share, i) for i in reversed(range(len(levels)))]

    gatherings = [gathering(p) for p in range(n)]
    crossings = [crossing(p) for p in range(n)]

    def cast(j, carry):
        half[j] = partial[1 - side, j].astype(bf16)
        return carry

    lax.fori_loop(0, pairs, cast, 0)
    greet(("seq", "head"))
    halving.start()
    gatherings[0].start()
    for p in range(n):
        gatherings[p].wait_recv()
        gatherings[p].wait_send()
        for later in (1, 2) if p == 0 else (p + 2,):
            if later < n:
                gatherings[later].start()

        def add(j, carry):
            total = got[p][0, j].astype(jnp.float32)
            for g in range(1, shards):
                total += got[p][g, j].astype(jnp.float32)
            summed[p][j] = total.astype(jnp.bfloat16)
            return carry

        def place(j, carry):
            returning[p][j] = summed[p][back[j]]
            return carry

        lax.fori_loop(0, requests, add, 0)
        lax.fori_loop(0, slots, place, 0)
        crossings[p].start()
        if p < len(actions):
            actions[p]()
    for action in actions[n:]:
        action()
    halving.wait_send()
    for level in levels:
        for copy in level[2] + level[4]:
            copy.wait_send()
    for p in range(n):
        crossings[p].wait_send()
        crossings[p].wait_recv()
    doubling.wait_send()
    doubled.wait_recv()


def semaphores(n, seq_count, shards):
    dma = pltpu.SemaphoreType.DMA
    return [
        dma((n, seq_count)),
        dma((n, seq_count)),
        dma((n,)),
        dma((n, shards)),
        dma((n, shards)),
        dma((n,)),
    ]


def fetch(pieces, capacity, seq_count, shards, picked, positions, pool):
    bf16 = jnp.bfloat16
    slots, requests = picked.shape[0], positions.shape[0]
    smem = pl.BlockSpec(memory_space=pltpu.SMEM)
    return pl.pallas_call(
        functools.partial(fetch_kernel, pieces, capacity),
        out_shape=[jax.ShapeDtypeStruct((shards, requests, p[1], p[3]), bf16) for p in pieces],
        in_specs=[smem, smem, pl.BlockSpec(memory_space=pltpu.VMEM)],
        out_specs=[pl.BlockSpec(memory_space=pl.ANY)] * len(pieces),
        scratch_shapes=[pltpu.VMEM((slots, p[1], p[3]), bf16) for p in pieces]
        + [pltpu.VMEM((slots, p[1], p[3]), bf16) for p in pieces]
        + [pltpu.VMEM((requests, p[1], p[3]), bf16) for p in pieces]
        + semaphores(len(pieces), seq_count, shards),
        compiler_params=pltpu.CompilerParams(
            collective_id=0, has_side_effects=True, vmem_limit_bytes=VMEM_LIMIT
        ),
        cost_estimate=pl.CostEstimate(
            flops=0, bytes_accessed=256 * 1024 * 1024, transcendentals=0
        ),
    )(picked, positions, pool)


def give_back(pieces, capacity, seq_count, shards, back, partial, shares):
    bf16 = jnp.bfloat16
    slots, requests = back.shape[0], shares[0].shape[1]
    hbm = pl.BlockSpec(memory_space=pl.ANY)
    vmem = pl.BlockSpec(memory_space=pltpu.VMEM)
    pairs, block = partial.shape[1], partial.shape[2:]
    dma = pltpu.SemaphoreType.DMA
    return pl.pallas_call(
        functools.partial(return_kernel, pieces, capacity),
        out_shape=[jax.ShapeDtypeStruct((slots, p[1], p[3]), bf16) for p in pieces]
        + [jax.ShapeDtypeStruct(partial.shape, bf16)],
        in_specs=[pl.BlockSpec(memory_space=pltpu.SMEM), vmem] + [hbm] * len(pieces),
        out_specs=[hbm] * len(pieces) + [vmem],
        scratch_shapes=[pltpu.VMEM((shards, requests, p[1], p[3]), bf16) for p in pieces]
        + [pltpu.VMEM((requests, p[1], p[3]), bf16) for p in pieces]
        + [pltpu.VMEM((slots, p[1], p[3]), bf16) for p in pieces]
        + semaphores(len(pieces), seq_count, shards)
        + [pltpu.VMEM((pairs,) + block, bf16)] * 3
        + [pltpu.VMEM((pairs,) + block, jnp.float32)]
        + [pltpu.VMEM((pairs.bit_length() - 1, pairs) + block, bf16)]
        + [dma((4,))]
        + [dma((pairs,))] * 4,
        compiler_params=pltpu.CompilerParams(
            collective_id=1, has_side_effects=True, vmem_limit_bytes=VMEM_LIMIT
        ),
        cost_estimate=pl.CostEstimate(
            flops=0, bytes_accessed=256 * 1024 * 1024, transcendentals=0
        ),
    )(back, partial, *shares)


def local(queries, pool, w_key, w_value, out_grad, nb_source, nb_slot, nb_count):
    f32 = jnp.float32
    bf16 = jnp.bfloat16
    seq_count = lax.axis_size("seq")
    seq_index = lax.axis_index("seq")
    shards = lax.axis_size("head")
    requests = CH_DEV * KNB
    capacity = max(2, 2 * requests // seq_count)
    slot_span = seq_count * capacity
    source_table = nb_source.reshape(seq_count, requests)
    slot_table = nb_slot.reshape(seq_count, requests)
    order_ids = jnp.arange(requests)
    matches = source_table[:, :, None] == source_table[:, None, :]
    before = order_ids[None, :] < order_ids[:, None]
    ranks = jnp.sum(jnp.logical_and(matches, before[None, :, :]), axis=2)
    places = jnp.arange(capacity)
    chosen = jnp.logical_and(
        (source_table == seq_index)[:, :, None], ranks[:, :, None] == places[None, None, :]
    )
    picked_slot = jnp.sum(jnp.where(chosen, slot_table[:, :, None], 0), axis=1).reshape(slot_span)
    filled = jnp.any(chosen, axis=1).reshape(slot_span)
    own_sources = lax.dynamic_index_in_dim(source_table, seq_index, 0, keepdims=False)
    own_ranks = lax.dynamic_index_in_dim(ranks, seq_index, 0, keepdims=False)
    positions = own_sources * capacity + own_ranks
    pool_count, rows, enc_width = pool.shape
    pieces = chunk_list(rows, enc_width)
    used_counts = lax.dynamic_slice_in_dim(nb_count, seq_index * CH_DEV, CH_DEV)

    panels = fetch(pieces, capacity, seq_count, shards, picked_slot, positions, pool)
    results = attention(
        pieces, shards, used_counts, queries, out_grad, w_key, w_value, panels
    )
    attended, grad_queries = results[:2]
    shares = results[2 : 2 + len(pieces)]
    partial = results[-1]
    blocks = partial.reshape(2, seq_count // 2, 2 * enc_width // seq_count, partial.shape[2])

    back = positions[None, :] == jnp.arange(slot_span)[:, None]
    back_index = jnp.sum(jnp.where(back, order_ids[None, :], 0), axis=1)
    collect = jnp.logical_and(
        picked_slot[None, :] == jnp.arange(pool_count)[:, None], filled[None, :]
    ).astype(bf16)
    *arrived, total = give_back(
        pieces, capacity, seq_count, shards, back_index, blocks, shares
    )
    grads = [
        jnp.einsum("pq,qre->pre", collect, part, preferred_element_type=f32) for part in arrived
    ]
    columns = len(COL_CUTS)
    grad_pool = jnp.concatenate(
        [
            jnp.concatenate(grads[cut * columns : (cut + 1) * columns], axis=2)
            for cut in range(len(pieces) // columns)
        ],
        axis=1,
    )
    grad_w_key, grad_w_value = total.reshape(partial.shape).astype(f32)
    return attended, grad_queries, grad_pool, grad_w_key, grad_w_value


def solution(mesh):
    return jax.shard_map(
        local,
        mesh=mesh,
        in_specs=(
            P("seq", "head"),
            P("seq", "head", None),
            P(None, "head"),
            P(None, "head"),
            P("seq", "head"),
            P(),
            P(),
            P(),
        ),
        out_specs=(
            P("seq", "head"),
            P("seq", "head"),
            P("seq", "head", None),
            P(None, "head"),
            P(None, "head"),
        ),
        check_vma=False,
    )
```
